256 devices in a mesh: sp: 64 (over z, x, core), batch: 4 (over y).
Axes of the slice: x: 4, y: 4, z: 8, core: 2. Of those that a mesh axis runs over, the one named last changes fastest.
Arguments:
- lifted_field: float32 [128, 128, 8192], P('batch', 'sp'), parts along dimension 0, may hold values from -6 to 6
- target_field: float32 [128, 32768], P('sp', 'batch'), parts along dimension 1, may hold values from -6 to 6
- spectral_one: float32 [2, 32, 512, 1024], P(None, None, 'sp'), may hold values from -5 to 5
- spectral_two: float32 [2, 32, 512, 1024], P(None, None, 'sp'), may hold values from -5 to 5
- pointwise_one: float32 [32, 32], replicated, may hold values from -1 to 1
- layer_bias_one: float32 [32], replicated, may hold values from -3 to 3
- pointwise_two: float32 [32, 32], replicated, may hold values from -1 to 1
- layer_bias_two: float32 [32], replicated, may hold values from -3 to 3
- hidden_weight: float32 [128, 32], replicated, may hold values from -1 to 1
- hidden_bias: float32 [128], replicated, may hold values from -3 to 3
- output_weight: float32 [128], replicated, may hold values from -4 to 4
Outputs:
- gradient_one: float32 [8, 32, 512, 1024], P('batch', None, 'sp'), parts along dimension 0
- gradient_two: float32 [8, 32, 512, 1024], P('batch', None, 'sp'), parts along dimension 0
The draws below stay inside these ranges and needn't reach their ends.
There are 4 independent parts, one for each index of `batch`. The reference program is written for one: setup_inputs(seed, part) draws one part's arguments, and reference() takes and returns one part's arrays. A program takes and returns all parts, laid end to end along the dimension named above; an argument that names none is the same for every part. Nothing has to cross between parts.
All inputs are finite; a program needn't handle non-finite values.
Results may differ from the reference program's by a relative error of at most 0.00018.
Values sent between devices are 32-bit elements; how exact they have to be, the bound alone decides.
No kernel may reach another device: no remote copies, remote signals or barrier semaphores. Data moves between devices by JAX's collectives and lax.ppermute only.
A program may use at most 128 MiB of HBM per device.

```python
import jax
import jax.numpy as jnp
from jax import lax

W = 32
H = 128
NX = 128
NY = 128
NZ = 64
KX = 32
KY = 32
KZ = 16


def block_levels(key, dims, shards, least, top_value):
    factor_of = 1.0
    for axis_at, blocks in shards:
        draws = jax.random.uniform(jax.random.fold_in(jax.random.fold_in(key, 6), axis_at), (blocks,), jnp.float32, least / len(shards), top_value / len(shards))
        factor_of = factor_of * jnp.repeat(jnp.exp(draws), dims[axis_at] // blocks).reshape((-1,) + (1,) * (len(dims) - 1 - axis_at))
    return factor_of


def bell_draw(stream_key, shape, scale, bound, cuts=(), kind=jnp.bfloat16):
    factor_of = block_levels(stream_key, shape, cuts, -0.22, 0.18) if cuts else 1.0
    result = jax.random.normal(stream_key, shape, jnp.float32) * scale * factor_of
    return jnp.minimum(jnp.maximum(result, -bound), bound).astype(kind)


def setup_inputs(seed: int = 0, part: int = 0) -> dict:
    streams_of = jax.random.split(jax.random.key(seed), 12)
    part_splits = jax.random.split(jax.random.fold_in(streams_of[11], part), 12)
    return {
        "lifted_field": bell_draw(part_splits[0], (W, NX, NY * NZ), 1.0, 6.0, ((1, 64),), jnp.float32),
        "target_field": bell_draw(part_splits[1], (NX, NY * NZ), 1.0, 6.0, ((0, 64),), jnp.float32),
        "spectral_one": bell_draw(streams_of[2], (2, KX, KY * KZ, W * W), 1.0, 5.0, ((2, 64),), jnp.float32),
        "spectral_two": bell_draw(streams_of[3], (2, KX, KY * KZ, W * W), 1.0, 5.0, ((2, 64),), jnp.float32),
        "pointwise_one": bell_draw(streams_of[4], (W, W), W ** -0.5, 1.0, (), jnp.float32),
        "layer_bias_one": bell_draw(streams_of[5], (W,), 0.5, 3.0, (), jnp.float32),
        "pointwise_two": bell_draw(streams_of[6], (W, W), W ** -0.5, 1.0, (), jnp.float32),
        "layer_bias_two": bell_draw(streams_of[7], (W,), 0.5, 3.0, (), jnp.float32),
        "hidden_weight": bell_draw(streams_of[8], (H, W), W ** -0.5, 1.0, (), jnp.float32),
        "hidden_bias": bell_draw(streams_of[9], (H,), 0.5, 3.0, (), jnp.float32),
        "output_weight": bell_draw(streams_of[10], (H,), 1.0, 4.0, (), jnp.float32),
    }


precise = lax.Precision.HIGHEST

def centred(number, length):
    indices = jnp.arange(number, dtype=jnp.int32)
    return jnp.where(indices < number // 2, indices, length - number + indices).astype(jnp.int32)

def spectral_term(layer_input, spectral):
    channels = layer_input.shape[0]
    coeffs = jnp.fft.rfftn(layer_input, axes=(1, 2, 3), norm='ortho')
    rows_x = centred(KX, NX)
    rows_y = centred(KY, NY)
    kept_modes = jnp.take(jnp.take(coeffs[..., :KZ], rows_x, axis=1), rows_y, axis=2)
    weights = lax.complex(spectral[0], spectral[1]).reshape(KX, KY, KZ, channels, channels)
    mixed = jnp.einsum('ixyz,xyzio->oxyz', kept_modes, weights, precision=precise)
    partial_y = jnp.zeros((channels, KX, NY, NZ // 2 + 1), mixed.dtype).at[:, :, rows_y, :KZ].set(mixed)
    padded = jnp.zeros((channels, NX, NY, NZ // 2 + 1), mixed.dtype).at[:, rows_x].set(partial_y)
    return jnp.fft.irfftn(padded, s=(NX, NY, NZ), axes=(1, 2, 3), norm='ortho')

def reference(lifted_field, target_field, spectral_one, spectral_two, pointwise_one, layer_bias_one, pointwise_two, layer_bias_two, hidden_weight, hidden_bias, output_weight):
    channels = lifted_field.shape[0]
    start_grid = lifted_field.reshape(channels, NX, NY, NZ)

    def apply_layer(layer_input, spectral, pointwise, layer_bias):
        local_term = jnp.einsum('oi,ixyz->oxyz', pointwise, layer_input, precision=precise)
        return jax.nn.gelu(spectral_term(layer_input, spectral) + local_term + layer_bias[:, None, None, None])

    def row_loss(row_pair):
        row_state, row_target = row_pair
        hidden = jax.nn.gelu(jnp.dot(hidden_weight, row_state, precision=precise, preferred_element_type=jnp.float32) + hidden_bias[:, None])
        predicted = jnp.dot(output_weight, hidden, precision=precise, preferred_element_type=jnp.float32)
        misfit = predicted - row_target
        return 0.5 * jnp.sum(misfit * misfit)

    def total_loss(first_weights, second_weights):
        layer_one = apply_layer(start_grid, first_weights, pointwise_one, layer_bias_one)
        layer_two = apply_layer(layer_one, second_weights, pointwise_two, layer_bias_two)
        rows_first = jnp.transpose(layer_two.reshape(channels, NX, NY * NZ), (1, 0, 2))
        return jnp.sum(lax.map(jax.checkpoint(row_loss), (rows_first, target_field)))
    _, pullback = jax.vjp(total_loss, spectral_one, spectral_two)
    gradient_one, gradient_two = pullback(jnp.ones((), lifted_field.dtype))
    return (gradient_one, gradient_two)
```

```python
import jax
import jax.numpy as jnp
import ml_dtypes
import numpy as np
from jax import lax
from jax.experimental import pallas as pl
from jax.experimental.pallas import tpu as pltpu
from jax.sharding import PartitionSpec as P

W = 32
H = 128
NX = 128
NY = 128
NZ = 64
KX = 32
KY = 32
KZ = 16

f32 = jnp.float32
bf16 = jnp.bfloat16
ROOT = 0.7978845608028654
CUBE = 0.044715 * ROOT


def centred(number, length):
    indices = np.arange(number)
    return np.where(indices < number // 2, indices, length - number + indices)


def two_parts(table):
    high = table.astype(ml_dtypes.bfloat16)
    low = (table - high.astype(np.float64)).astype(ml_dtypes.bfloat16)
    return high, low


def across_table():
    y = 2 * np.arange(64)[None, :] + np.arange(2)[:, None]
    angle = 2 * np.pi * (centred(KY, NY)[:, None, None] * y[None] % NY) / NY
    waves = np.stack([np.cos(angle), -np.sin(angle)])
    return np.einsum("skab,rt->srkabt", waves, np.eye(2)).reshape(128, 256)


def rotation(angle):
    cosine, sine = np.cos(angle), np.sin(angle)
    return np.stack([np.stack([cosine, -sine]), np.stack([sine, cosine])])


def depth_table(channel_major):
    angle = 2 * np.pi * (np.arange(NZ)[:, None] * np.arange(KZ)[None] % NZ) / NZ
    form = "zk,cd->czkd" if channel_major else "zk,cd->zckd"
    return [np.einsum(form, wave(angle), np.eye(16)).reshape(1024, 256) for wave in (np.cos, np.sin)]


def first_table():
    places = 2 * np.arange(64)[:, None] + np.arange(2)[None]
    angle = 2 * np.pi * (centred(KX, NX)[:, None, None] * places[None] % NX) / NX
    table = np.einsum("stkdr,gh->gtkdrsh", rotation(angle), np.eye(2))
    return table.reshape(128, 512) / 1024.0


def selectors():
    eye16, eye32 = np.eye(16), np.eye(32)
    lanes = np.zeros((128, 32))
    lanes[:32] = eye32
    spread = np.einsum("li,o->lio", lanes, np.ones(32)).reshape(128, 1024)
    tile = np.einsum("lo,i->lio", lanes, np.ones(4)).reshape(128, 128)
    halves = eye32.reshape(32, 2, 16)
    gather = np.einsum("i,ogc,k->iogkc", np.ones(4), halves, np.ones(8)).reshape(128, 256)
    gather_rows = np.einsum("igc,o,k->iogkc", halves, np.ones(32), np.ones(8)).reshape(1024, 256)
    return [part.astype(ml_dtypes.bfloat16) for part in (spread, tile, gather, gather_rows)]


def head_selectors():
    one = ml_dtypes.bfloat16
    channels = np.einsum("z,igc->gzci", np.ones(8), np.eye(32).reshape(32, 2, 16)).reshape(256, 32)
    hidden = np.einsum("hbu,z->hbzu", np.eye(128).reshape(128, 8, 16), np.ones(8)).reshape(128, 1024)
    ones = np.einsum("zy,uc->zuyc", np.eye(8), np.ones((16, 16))).reshape(128, 128)
    cells = np.einsum("ab,zy,c->bzayc", np.eye(2), np.eye(64), np.ones(16)).reshape(128, 2048)
    return channels.astype(one), hidden.astype(one), ones.astype(one), cells.astype(one)


def turn_table():
    return np.einsum("zy,cd->czyd", np.eye(64), np.eye(16)).reshape(1024, 1024).astype(ml_dtypes.bfloat16)


def split(values):
    high = values.astype(bf16)
    return high, (values - high.astype(f32)).astype(bf16)


def dot(left, right):
    return lax.dot_general(left, right, (((1,), (0,)), ((), ())), preferred_element_type=f32)


def dot_t(left, right):
    return lax.dot_general(left, right, (((1,), (1,)), ((), ())), preferred_element_type=f32)


def dot3(left, right, product=dot):
    return product(left[0], right[0]) + (product(left[1], right[0]) + product(left[0], right[1]))


def run(body, name, flops, near, far, outs, scratch):
    leaving = [k for k, out in enumerate(outs) if out[2] == "far"]

    def kernel(*refs):
        refs = list(refs)
        take = lambda count: [refs.pop(0) for _ in range(count)]
        near_refs, far_refs, out_refs = take(len(near)), take(len(far)), take(len(outs))
        copied, filled = take(len(far)), take(len(leaving))
        scratch_refs = take(len(scratch))
        arrived, left = refs
        copies = [pltpu.make_async_copy(a, b, arrived.at[k]) for k, (a, b) in enumerate(zip(far_refs, copied))]
        for copy in copies:
            copy.start()
        waited, started = set(), []

        def fetch(k):
            if k not in waited:
                copies[k].wait()
                waited.add(k)
            return copied[k]

        def put(k):
            index = leaving.index(k)
            copy = pltpu.make_async_copy(filled[index], out_refs[k], left.at[index])
            copy.start()
            started.append(copy)

        shown = [filled[leaving.index(k)] if k in leaving else out for k, out in enumerate(out_refs)]
        body(near_refs, fetch, shown, put, scratch_refs)
        for k in range(len(far)):
            fetch(k)
        for copy in started:
            copy.wait()

    far = [pltpu.with_memory_space_constraint(o, pltpu.HBM) for o in far]
    vmem, hbm = pl.BlockSpec(memory_space=pltpu.VMEM), pl.BlockSpec(memory_space=pltpu.HBM)
    moved = sum(o.size * o.dtype.itemsize for o in (*near, *far))
    return pl.pallas_call(
        kernel,
        in_specs=[vmem] * len(near) + [hbm] * len(far),
        out_specs=[hbm if out[2] == "far" else vmem for out in outs],
        out_shape=[pltpu.HBM(out[0], out[1]) if out[2] == "far" else jax.ShapeDtypeStruct(out[0], out[1]) for out in outs],
        scratch_shapes=[pltpu.VMEM(o.shape, o.dtype) for o in far]
        + [pltpu.VMEM(outs[k][0], outs[k][1]) for k in leaving]
        + scratch
        + [pltpu.SemaphoreType.DMA((max(1, len(far)),)), pltpu.SemaphoreType.DMA((max(1, len(leaving)),))],
        name=name,
        cost_estimate=pl.CostEstimate(flops=flops, bytes_accessed=int(moved), transcendentals=0),
        compiler_params=pltpu.CompilerParams(vmem_limit_bytes=48 * 1024 * 1024),
    )(*near, *far)


def spectra_of(turned, depth):
    rows = [turned[s * 64 : s * 64 + 64, g * 1024 : g * 1024 + 1024] for s in range(2) for g in range(2)]
    left = split(jnp.concatenate(rows, 0))
    even = dot3(left, (depth[0][...], depth[1][...]))
    odd = dot3(left, (depth[2][...], depth[3][...]))
    return even[:128] + odd[128:], even[128:] - odd[:128]


def place_modes(spectra, send_ref):
    for p in range(2):
        for g in range(2):
            for r in range(2):
                for kzh in range(2):
                    row = g * 64 + r * 32
                    send_ref[pl.ds(kzh * 8 + r * 4 + p * 2 + g, 32, stride=16), :] = spectra[p][
                        row : row + 32, kzh * 128 : kzh * 128 + 128
                    ]


def send_modes(parts, across, depth, send_ref):
    turned = dot3((across[0][...], across[1][...]), parts)
    place_modes(spectra_of(turned, depth), send_ref)


def taken_rows(recv_ref):
    rows = []
    for p in range(2):
        for g in range(2):
            for r in range(2):
                pieces = [recv_ref[pl.ds(kzh * 8 + r * 4 + p * 2 + g, 32, stride=16), :] for kzh in range(2)]
                rows.append(jnp.concatenate(pieces, 1))
    return split(jnp.concatenate(rows, 0))


def cells_from(recv_ref, back, depth):
    left = taken_rows(recv_ref)
    depth = [depth(k) for k in range(4)]
    even = dot3(left, (depth[0][...], depth[1][...]), dot_t)
    odd = dot3(left, (depth[2][...], depth[3][...]), dot_t)
    real, imag = even[:128] - odd[128:], odd[:128] + even[128:]
    rows = [jnp.concatenate([part[:64], part[64:]], 1) for part in (real, imag)]
    back = [back(k) for k in range(2)]
    return dot3((back[0][...], back[1][...]), split(jnp.concatenate(rows, 0)))


def plain_rows(field_ref, g):
    low_rows, high_rows = [], []
    lane = lax.broadcasted_iota(jnp.int32, (128, 128), 1) < 64
    for pair in range(8):
        first = field_ref[g * 16 + 2 * pair]
        second = field_ref[g * 16 + 2 * pair + 1]
        low_rows.append(jnp.where(lane, first, pltpu.roll(second, 64, 1)))
        high_rows.append(jnp.where(lane, pltpu.roll(first, 64, 1), second))
    return jnp.concatenate([jnp.concatenate(low_rows, 1), jnp.concatenate(high_rows, 1)], 0)


def lift_body(near, fetch, outs, put, scratch):
    field_ref = fetch(0)
    parts = [split(plain_rows(field_ref, g)) for g in range(2)]
    parts = tuple(jnp.concatenate([parts[0][k], parts[1][k]], 1) for k in range(2))
    turned = dot3((fetch(1)[...], fetch(2)[...]), parts)
    place_modes(spectra_of(turned, [fetch(k) for k in range(3, 7)]), outs[0])


def point_chunks(parts_at, mix, bias, out_ref):
    for q in range(8):
        mixed = dot3(parts_at(q), mix) + bias
        out_ref[:, q * 128 : q * 128 + 128] = mixed[:, :128]
        out_ref[:, 1024 + q * 128 : 1152 + q * 128] = mixed[:, 128:]


def both(value, q):
    return jnp.concatenate([value[:, q * 128 : q * 128 + 128], value[:, 1024 + q * 128 : 1152 + q * 128]], 1)


def lift_point_body(near, fetch, outs, put, scratch):
    turned = []
    for g in range(2):
        high, low = split(plain_rows(fetch(0), g))
        turned.append((dot(high, fetch(1)[...]).astype(bf16), dot(low, fetch(1)[...]).astype(bf16)))
    parts = tuple(jnp.concatenate([turned[0][k], turned[1][k]], 1) for k in range(2))
    mix, bias = (fetch(2)[...], fetch(3)[...]), fetch(4)[:1, :]
    point_chunks(lambda q: tuple(both(part, q) for part in parts), mix, bias, outs[0])
    put(0)


def point_body(near, fetch, outs, put, scratch):
    mix, bias = (fetch(1)[...], fetch(2)[...]), fetch(3)[:1, :]
    state_ref = fetch(0)
    point_chunks(lambda q: split(both(state_ref, q)), mix, bias, outs[0])
    put(0)


def gelu_parts(x):
    square = x * x
    cubic = square * CUBE
    bend = jnp.tanh(x * (cubic + ROOT))
    above = bend + 1.0
    twice = x * above
    slope = above + (twice * (1.0 - bend)) * (cubic * 3.0 + ROOT)
    return twice, slope


def tiles(body, rows=16, lanes=512, height=256, width=2048):
    def step(index, carry):
        start = pl.multiple_of(index * rows, rows)
        for column in range(0, width, lanes):
            body(pl.ds(start, rows), slice(column, column + lanes))
        return carry

    lax.fori_loop(0, height // rows, step, 0)


def one_body(near, fetch, outs, put, scratch):
    send_ref, state_ref, slope_ref = outs
    pre, high, low = scratch
    pre[...] = cells_from(near[0], lambda k: fetch(4 + k), fetch)
    local_ref = fetch(6)

    def body(rows, columns):
        twice, slope = gelu_parts(pre[rows, columns] + local_ref[rows, columns])
        state = 0.5 * twice
        state_ref[rows, columns] = state
        slope_ref[rows, columns] = 0.5 * slope
        high[rows, columns], low[rows, columns] = split(state)

    tiles(body)
    put(1)
    put(2)
    send_modes((high[...], low[...]), [fetch(7), fetch(8)], [fetch(k) for k in range(4)], send_ref)


def two_body(near, fetch, outs, put, scratch):
    send_ref, back_ref = outs
    pre, high, low, hidden, slope_h, slope_l, sums = scratch
    pre[...] = cells_from(near[0], lambda k: fetch(4 + k), fetch)
    local_ref = fetch(6)

    def body(rows, columns):
        twice, slope = gelu_parts(pre[rows, columns] + local_ref[rows, columns])
        pre[rows, columns] = 0.5 * slope
        high[rows, columns], low[rows, columns] = split(0.5 * twice)

    tiles(body)
    up_h, up_l, rows_ref, down_h, down_l, ones_ref, target_ref = [fetch(k) for k in range(9, 16)]

    def chunk(q, carry):
        first = pl.ds(pl.multiple_of(q * 128, 128), 128)
        second = pl.ds(pl.multiple_of(1024 + q * 128, 128), 128)
        left = tuple(jnp.concatenate([part[:, first], part[:, second]], 1) for part in (high, low))
        hidden[...] = dot3(left, (up_h[...], up_l[...]))

        def strip(index, inner):
            rows = pl.ds(pl.multiple_of(index * 16, 16), 16)
            total = jnp.zeros((16, 128), f32)
            for b in range(8):
                columns = slice(b * 128, b * 128 + 128)
                twice, slope = gelu_parts(hidden[rows, columns] + rows_ref[0:16, columns])
                total = total + twice * rows_ref[16:32, columns]
                slope_h[rows, columns], slope_l[rows, columns] = split(slope)
            sums[rows, :128], sums[rows, 128:] = split(total)
            return inner

        lax.fori_loop(0, 16, strip, 0)
        reach = dot3((slope_h[...], slope_l[...]), (down_h[...], down_l[...]), dot_t)
        misfit = dot(sums[:, :128], ones_ref[...]) + dot(sums[:, 128:], ones_ref[...]) - target_ref[:, first]
        for part, columns in ((0, first), (1, second)):
            back = pre[:, columns] * (misfit * reach[:, part * 128 : part * 128 + 128])
            back_ref[:, columns] = back
            high[:, columns], low[:, columns] = split(back)
        return carry

    lax.fori_loop(0, 8, chunk, 0)
    put(1)
    send_modes((high[...], low[...]), [fetch(7), fetch(8)], [fetch(k) for k in range(4)], send_ref)


def back_body(near, fetch, outs, put, scratch):
    pre, high, low = scratch
    pre[...] = cells_from(near[0], lambda k: fetch(4 + k), fetch)
    local_ref, slope_ref = fetch(6), fetch(9)

    def body(rows, columns):
        back = slope_ref[rows, columns] * (pre[rows, columns] + local_ref[rows, columns])
        high[rows, columns], low[rows, columns] = split(back)

    tiles(body)
    send_modes((high[...], low[...]), [fetch(7), fetch(8)], [fetch(k) for k in range(4)], outs[0])


def mode_rows(recv_ref, first, factor, rows_ref):
    spectrum = dot3((first[0][...], first[1][...]), split(recv_ref[...]))
    if factor is not None:
        spectrum = spectrum * factor
    lane = lax.broadcasted_iota(jnp.int32, (64, 128), 1)
    for kz in range(8):
        first = spectrum[:64] if kz == 0 else pltpu.roll(spectrum[:64], 128 - 16 * kz, 1)
        second = spectrum[64:] if kz == 1 else pltpu.roll(spectrum[64:], (144 - 16 * kz) % 128, 1)
        joined = jnp.where(lane < 16, first, jnp.where(lane < 32, second, 0.0))
        rows_ref[pl.ds(kz, 64, stride=8), :] = joined


def selected(rows_ref, table):
    high, low = split(rows_ref[...])
    return dot(high, table[...]) + dot(low, table[...])


def send_cells(sums_ref, factor, first_back, send_ref):
    kz_lane = lax.broadcasted_iota(jnp.int32, (64, 128), 1) // 16
    packed = [jnp.zeros((64, 128), f32) for _ in range(2)]
    for kz in range(8):
        for g in range(2):
            packed[g] = jnp.where(kz_lane == kz, sums_ref[pl.ds(g * 512 + kz, 64, stride=8), :], packed[g])
    joined = jnp.concatenate(packed, 0)
    if factor is not None:
        joined = joined * factor
    send_ref[...] = dot3((first_back[0][...], first_back[1][...]), split(joined))


def mix_body(near, fetch, outs, put, scratch):
    send_ref, rows_ref = outs
    wide, sums, out = scratch
    mode_rows(near[0], [fetch(0), fetch(1)], None, rows_ref)
    put(1)
    wide[...] = selected(rows_ref, fetch(3))
    weight_ref = fetch(4)

    def step(kx, carry):
        real = pl.ds(pl.multiple_of(kx * 8, 8), 8)
        imag = pl.ds(pl.multiple_of(256 + kx * 8, 8), 8)
        total_real = jnp.zeros((8, 128), f32)
        total_imag = jnp.zeros((8, 128), f32)
        for b in range(8):
            columns = slice(b * 128, b * 128 + 128)
            fr, fi = wide[real, columns], wide[imag, columns]
            wr, wi = weight_ref[real, columns], weight_ref[imag, columns]
            total_real = total_real + (fr * wr - fi * wi)
            total_imag = total_imag + (fr * wi + fi * wr)
        sums[real, :] = total_real
        sums[imag, :] = total_imag
        return carry

    lax.fori_loop(0, 32, step, 0, unroll=4)
    mixed = selected(sums, fetch(5))
    out[:512, :] = mixed[:, :128]
    out[512:, :] = mixed[:, 128:]
    send_cells(out, fetch(2)[:1, :], [fetch(6), fetch(7)], send_ref)


def adjoint_body(near, fetch, outs, put, scratch):
    send_ref, rows_ref = outs
    wide, high, low, out = scratch
    mode_rows(near[0], [fetch(0), fetch(1)], fetch(2)[:1, :], rows_ref)
    put(1)
    wide[...] = selected(rows_ref, fetch(3))
    weight_ref = fetch(4)

    def step(kx, carry):
        real = pl.ds(pl.multiple_of(kx * 16, 16), 16)
        imag = pl.ds(pl.multiple_of(256 + kx * 16, 16), 16)
        br, bi = wide[real, :], wide[imag, :]
        for b in range(8):
            columns = slice(b * 128, b * 128 + 128)
            wr, wi = weight_ref[real, columns], weight_ref[imag, columns]
            high[real, columns], low[real, columns] = split(br * wr + bi * wi)
            high[imag, columns], low[imag, columns] = split(bi * wr - br * wi)
        return carry

    lax.fori_loop(0, 16, step, 0)
    table = fetch(5)[...]
    mixed = dot(high[...], table) + dot(low[...], table)
    out[:512, :] = mixed[:, :128]
    out[512:, :] = mixed[:, 128:]
    send_cells(out, None, [fetch(6), fetch(7)], send_ref)


def outer_products(forward_ref, back_ref, spread_ref, tile_ref, grad_ref, wide, narrow):
    wide[...] = selected(forward_ref, spread_ref)
    narrow[...] = selected(back_ref, tile_ref)

    def step(kx, carry):
        real = pl.ds(pl.multiple_of(kx * 8, 8), 8)
        imag = pl.ds(pl.multiple_of(256 + kx * 8, 8), 8)
        br, bi = narrow[real, :], narrow[imag, :]
        for b in range(8):
            columns = slice(b * 128, b * 128 + 128)
            fr, fi = wide[real, columns], wide[imag, columns]
            grad_ref[real, columns] = fr * br + fi * bi
            grad_ref[imag, columns] = fr * bi - fi * br
        return carry

    lax.fori_loop(0, 32, step, 0, unroll=4)


def grad_body(near, fetch, outs, put, scratch):
    outer_products(fetch(0), fetch(1), fetch(2), fetch(3), outs[0], *scratch)
    put(0)


def last_body(near, fetch, outs, put, scratch):
    rows, wide, narrow = scratch
    mode_rows(near[0], [fetch(0), fetch(1)], fetch(2)[:1, :], rows)
    outer_products(fetch(3), rows, fetch(4), fetch(5), outs[0], wide, narrow)
    put(0)


def table_body(near, fetch, outs, put, scratch):
    point_one, point_two, hidden_t, vectors, biases, target, channels, hidden, cells = [fetch(k) for k in range(9)]
    one_h, one_l, two_h, two_l, back_h, back_l, up_h, up_l, down_h, down_l, rows_ref, bias_one, bias_two, target_ref = outs
    z_row = lax.broadcasted_iota(jnp.int32, (256, 1024), 0) // 16 % 8
    z_column = lax.broadcasted_iota(jnp.int32, (256, 1024), 1) // 16 % 8
    same = z_row == z_column

    def widen(left, right, mask, high, low):
        for part, out in zip(split(left), (high, low)):
            rows = dot(channels[...], part).astype(bf16)
            out[...] = jnp.where(mask, right(rows), 0.0).astype(bf16)

    square = same[:, :256]
    to_channels = lambda rows: dot_t(rows, channels[...])
    to_hidden = lambda rows: dot(rows, hidden[...])
    widen(point_one[...].T, to_channels, square, one_h, one_l)
    widen(point_two[...].T, to_channels, square, two_h, two_l)
    widen(point_two[...], to_channels, square, back_h, back_l)
    widen(hidden_t[...], to_hidden, same, up_h, up_l)
    widen(hidden_t[...] * (0.5 * vectors[1:2, :]), to_hidden, same, down_h, down_l)

    def exact(values, product):
        high, low = split(values)
        last = (values - high.astype(f32) - low.astype(f32)).astype(bf16)
        return product(high) + (product(low) + product(last))

    rows_ref[0:16, :] = exact(jnp.broadcast_to(vectors[0:1, :], (16, 128)), to_hidden)
    rows_ref[16:32, :] = exact(jnp.broadcast_to(0.5 * vectors[1:2, :], (16, 128)), to_hidden)
    bias_one[...] = exact(jnp.broadcast_to(biases[0:1, :], (8, 32)), to_channels)
    bias_two[...] = exact(jnp.broadcast_to(biases[1:2, :], (8, 32)), to_channels)
    spread = exact(target[...], lambda part: dot(part, cells[...]))
    target_ref[:128, :] = spread[:, :1024]
    target_ref[128:, :] = spread[:, 1024:]
    for k in range(14):
        put(k)


def shards(
    lifted_field,
    target_field,
    spectral_one,
    spectral_two,
    pointwise_one,
    layer_bias_one,
    pointwise_two,
    layer_bias_two,
    hidden_weight,
    hidden_bias,
    output_weight,
):
    across = tuple(map(jnp.asarray, two_parts(across_table())))
    across_back = tuple(map(jnp.asarray, two_parts(np.ascontiguousarray(across_table().T))))
    depth, depth_lifted = (
        tuple(jnp.asarray(part) for wave in depth_table(major) for part in two_parts(wave)) for major in (False, True)
    )
    first = tuple(map(jnp.asarray, two_parts(first_table())))
    first_back = tuple(map(jnp.asarray, two_parts(np.ascontiguousarray(first_table().T))))
    spread, tile, gather, gather_rows = map(jnp.asarray, selectors())
    channels, hidden, ones, cells = map(jnp.asarray, head_selectors())
    turn = jnp.asarray(turn_table())

    field = lifted_field.reshape(W, 2, 64, 128).transpose(0, 2, 1, 3).reshape(W, 128, 128)
    target = target_field.reshape(2, 64, 128).transpose(1, 0, 2).reshape(128, 128)
    weights_one = spectral_one.reshape(512, 1024)
    weights_two = spectral_two.reshape(512, 1024)
    mine = lax.axis_index("sp")
    lane = jnp.arange(128, dtype=jnp.int32)[None, :]
    factor = jnp.broadcast_to(jnp.where((lane < 16) & (mine % 2 == 0), 1.0, 2.0), (8, 128)).astype(f32)

    def exchange(blocks):
        moved = lax.all_to_all(blocks.reshape(64, 8, 128), "sp", split_axis=0, concat_axis=0, tiled=True)
        return moved.reshape(512, 128)

    block, grid, wide = (512, 128), (256, 2048), (512, 1024)
    vm = pltpu.VMEM
    near_out = (block, f32, "near")
    far_out = lambda shape, kind=f32: (shape, kind, "far")
    work = [vm(grid, f32), vm(grid, bf16), vm(grid, bf16)]
    mix_work = [vm(wide, f32), vm(block, f32), vm((1024, 128), f32)]

    (send,) = run(lift_body, "lift", 2 * 10**9, (), (field, *across, *depth_lifted), [near_out], [])
    recv = exchange(send)
    made = run(
        table_body, "tables", 3 * 10**9, (),
        (
            pointwise_one, pointwise_two, hidden_weight.T, jnp.stack([hidden_bias, output_weight]),
            jnp.stack([layer_bias_one, layer_bias_two]), target, channels, hidden, cells,
        ),
        [far_out((256, 256), bf16)] * 6 + [far_out((256, 1024), bf16)] * 4
        + [far_out((32, 1024)), far_out((8, 256)), far_out((8, 256)), far_out((256, 1024))],
        [],
    )
    mix_one, mix_two, mix_back = made[0:2], made[2:4], made[4:6]
    up, down = made[6:8], made[8:10]
    hidden_rows, bias_one, bias_two, target_wide = made[10:]
    (local_one,) = run(lift_point_body, "lift_point", 4 * 10**9, (), (field, turn, *mix_one, bias_one), [far_out(grid)], [])
    send, modes_one = run(
        mix_body, "mix_one", 10**9, (recv,), (*first, factor, spread, weights_one, gather, *first_back),
        [near_out, far_out(block)], mix_work,
    )
    recv = exchange(send)
    send, state_one, slope_one = run(
        one_body, "grid_one", 5 * 10**9, (recv,), (*depth, *across_back, local_one, *across),
        [near_out, far_out(grid), far_out(grid)], work,
    )
    recv = exchange(send)
    (local_two,) = run(point_body, "point_two", 10**9, (), (state_one, *mix_two, bias_two), [far_out(grid)], [])
    send, modes_two = run(
        mix_body, "mix_two", 10**9, (recv,), (*first, factor, spread, weights_two, gather, *first_back),
        [near_out, far_out(block)], mix_work,
    )
    recv = exchange(send)
    send, back_two = run(
        two_body, "grid_two", 15 * 10**9, (recv,),
        (*depth, *across_back, local_two, *across, *up, hidden_rows, *down, ones, target_wide),
        [near_out, far_out(grid)],
        work + [vm((256, 1024), f32), vm((256, 1024), bf16), vm((256, 1024), bf16), vm((256, 256), bf16)],
    )
    recv = exchange(send)
    no_bias = jnp.zeros((8, 256), f32)
    (local_back,) = run(point_body, "point_back", 10**9, (), (back_two, *mix_back, no_bias), [far_out(grid)], [])
    send, modes_back = run(
        adjoint_body, "adjoint", 10**9, (recv,), (*first, factor, tile, weights_two, gather_rows, *first_back),
        [near_out, far_out(block)], [vm(block, f32), vm(wide, bf16), vm(wide, bf16), vm((1024, 128), f32)],
    )
    recv = exchange(send)
    (gradient_two,) = run(
        grad_body, "grad_two", 10**9, (), (modes_two, modes_back, spread, tile), [far_out(wide)], [vm(wide, f32), vm(block, f32)]
    )
    (send,) = run(
        back_body, "grid_back", 5 * 10**9, (recv,), (*depth, *across_back, local_back, *across, slope_one), [near_out], work
    )
    recv = exchange(send)
    (gradient_one,) = run(
        last_body, "grad_one", 10**9, (recv,), (*first, factor, modes_one, spread, tile), [far_out(wide)],
        [vm(block, f32), vm(wide, f32), vm(block, f32)],
    )
    shape = (2, KX, 8, W * W)
    return (gradient_one.reshape(shape), gradient_two.reshape(shape))


def solution(mesh):
    in_specs = (
        P("batch", "sp", None),
        P("sp", "batch"),
        P(None, None, "sp", None),
        P(None, None, "sp", None),
        P(),
        P(),
        P(),
        P(),
        P(),
        P(),
        P(),
    )
    out_specs = (P("batch", None, "sp", None), P("batch", None, "sp", None))
    return jax.shard_map(shards, mesh=mesh, in_specs=in_specs, out_specs=out_specs, check_vma=False)
```

```python
import jax
import jax.numpy as jnp
import ml_dtypes
import numpy as np
from jax import lax
from jax.experimental import pallas as pl
from jax.experimental.pallas import tpu as pltpu
from jax.sharding import PartitionSpec as P

W = 32
H = 128
NX = 128
NY = 128
NZ = 64
KX = 32
KY = 32
KZ = 16

f32 = jnp.float32
bf16 = jnp.bfloat16
ROOT = 0.7978845608028654
CUBE = 0.044715 * ROOT


def centred(number, length):
    indices = np.arange(number)
    return np.where(indices < number // 2, indices, length - number + indices)


def two_parts(table):
    high = table.astype(ml_dtypes.bfloat16)
    low = (table - high.astype(np.float64)).astype(ml_dtypes.bfloat16)
    return high, low


def across_table():
    y = 2 * np.arange(64)[None, :] + np.arange(2)[:, None]
    angle = 2 * np.pi * (centred(KY, NY)[:, None, None] * y[None] % NY) / NY
    waves = np.stack([np.cos(angle), -np.sin(angle)])
    return np.einsum("skab,rt->srkabt", waves, np.eye(2)).reshape(128, 256)


def rotation(angle):
    cosine, sine = np.cos(angle), np.sin(angle)
    return np.stack([np.stack([cosine, -sine]), np.stack([sine, cosine])])


def depth_table(channel_major):
    angle = 2 * np.pi * (np.arange(NZ)[:, None] * np.arange(KZ)[None] % NZ) / NZ
    form = "zk,cd->czkd" if channel_major else "zk,cd->zckd"
    return [np.einsum(form, wave(angle), np.eye(16)).reshape(1024, 256) for wave in (np.cos, np.sin)]


def first_table():
    places = 2 * np.arange(64)[:, None] + np.arange(2)[None]
    angle = 2 * np.pi * (centred(KX, NX)[:, None, None] * places[None] % NX) / NX
    table = np.einsum("stkdr,gh->gtkdrsh", rotation(angle), np.eye(2))
    return table.reshape(128, 512) / 1024.0


def selectors():
    eye16, eye32 = np.eye(16), np.eye(32)
    lanes = np.zeros((128, 32))
    lanes[:32] = eye32
    spread = np.einsum("li,o->lio", lanes, np.ones(32)).reshape(128, 1024)
    tile = np.einsum("lo,i->lio", lanes, np.ones(4)).reshape(128, 128)
    halves = eye32.reshape(32, 2, 16)
    gather = np.einsum("i,ogc,k->iogkc", np.ones(4), halves, np.ones(8)).reshape(128, 256)
    gather_rows = np.einsum("igc,o,k->iogkc", halves, np.ones(32), np.ones(8)).reshape(1024, 256)
    return [part.astype(ml_dtypes.bfloat16) for part in (spread, tile, gather, gather_rows)]


def head_selectors():
    one = ml_dtypes.bfloat16
    channels = np.einsum("z,igc->gzci", np.ones(8), np.eye(32).reshape(32, 2, 16)).reshape(256, 32)
    hidden = np.einsum("hbu,z->hbzu", np.eye(128).reshape(128, 8, 16), np.ones(8)).reshape(128, 1024)
    ones = np.einsum("zy,uc->zuyc", np.eye(8), np.ones((16, 16))).reshape(128, 128)
    cells = np.einsum("ab,zy,c->bzayc", np.eye(2), np.eye(64), np.ones(16)).reshape(128, 2048)
    return channels.astype(one), hidden.astype(one), ones.astype(one), cells.astype(one)


def turn_table():
    return np.einsum("zy,cd->czyd", np.eye(64), np.eye(16)).reshape(1024, 1024).astype(ml_dtypes.bfloat16)


def split(values):
    high = values.astype(bf16)
    return high, (values - high.astype(f32)).astype(bf16)


def dot(left, right):
    return lax.dot_general(left, right, (((1,), (0,)), ((), ())), preferred_element_type=f32)


def dot_t(left, right):
    return lax.dot_general(left, right, (((1,), (1,)), ((), ())), preferred_element_type=f32)


def dot3(left, right, product=dot):
    return product(left[0], right[0]) + (product(left[1], right[0]) + product(left[0], right[1]))


def run(body, name, flops, near, far, outs, scratch, parts={}, managed=False):
    if managed:
        outs = [(shape, kind, "near") for shape, kind, _ in outs]
    leaving = [k for k, out in enumerate(outs) if out[2] == "far"]

    def kernel(*refs):
        refs = list(refs)
        take = lambda count: [refs.pop(0) for _ in range(count)]
        near_refs, far_refs, out_refs = take(len(near)), take(len(far)), take(len(outs))
        copied, filled = take(0 if managed else len(far)), take(len(leaving))
        scratch_refs = take(len(scratch))
        arrived, left = refs
        for k, (start, stop) in parts.items():
            far_refs[k] = far_refs[k].at[pl.ds(start, stop - start)]
        copies = [pltpu.make_async_copy(a, b, arrived.at[k]) for k, (a, b) in enumerate(zip(far_refs, copied))]
        for copy in copies:
            copy.start()
        waited, started = set(), []

        def fetch(k):
            if managed:
                return far_refs[k]
            if k not in waited:
                copies[k].wait()
                waited.add(k)
            return copied[k]

        def put(k, rows=None):
            if managed:
                return
            source, target = filled[leaving.index(k)], out_refs[k]
            if rows is not None:
                source, target = source.at[rows], target.at[rows]
            copy = pltpu.make_async_copy(source, target, left.at[len(started)])
            copy.start()
            started.append(copy)

        shown = [filled[leaving.index(k)] if k in leaving else out for k, out in enumerate(out_refs)]
        body(near_refs, fetch, shown, put, scratch_refs)
        for k in range(len(far)):
            fetch(k)
        for copy in started:
            copy.wait()

    if not managed:
        far = [pltpu.with_memory_space_constraint(o, pltpu.HBM) for o in far]
    vmem, hbm = pl.BlockSpec(memory_space=pltpu.VMEM), pl.BlockSpec(memory_space=pltpu.HBM)
    moved = sum(o.size * o.dtype.itemsize for o in (*near, *far))
    return pl.pallas_call(
        kernel,
        in_specs=[vmem] * len(near) + [vmem if managed else hbm] * len(far),
        out_specs=[hbm if out[2] == "far" else vmem for out in outs],
        out_shape=[pltpu.HBM(out[0], out[1]) if out[2] == "far" else jax.ShapeDtypeStruct(out[0], out[1]) for out in outs],
        scratch_shapes=[
            pltpu.VMEM((parts[k][1] - parts[k][0], *o.shape[1:]) if k in parts else o.shape, o.dtype)
            for k, o in enumerate(far)
            if not managed
        ]
        + [pltpu.VMEM(outs[k][0], outs[k][1]) for k in leaving]
        + scratch
        + [pltpu.SemaphoreType.DMA((max(1, len(far)),)), pltpu.SemaphoreType.DMA((16,))],
        name=name,
        cost_estimate=pl.CostEstimate(flops=flops, bytes_accessed=int(moved), transcendentals=0),
        compiler_params=pltpu.CompilerParams(vmem_limit_bytes=28 * 1024 * 1024),
    )(*near, *far)


def spectra_of(turned, depth):
    rows = [turned[s * 64 : s * 64 + 64, g * 1024 : g * 1024 + 1024] for s in range(2) for g in range(2)]
    left = split(jnp.concatenate(rows, 0))
    even = dot3(left, (depth[0][...], depth[1][...]))
    odd = dot3(left, (depth[2][...], depth[3][...]))
    return even[:128] + odd[128:], even[128:] - odd[:128]


def place_modes(spectra, send_ref):
    for p in range(2):
        for g in range(2):
            for r in range(2):
                for kzh in range(2):
                    row = g * 64 + r * 32
                    send_ref[pl.ds(kzh * 8 + r * 4 + p * 2 + g, 32, stride=16), :] = spectra[p][
                        row : row + 32, kzh * 128 : kzh * 128 + 128
                    ]


def send_modes(parts, across, depth, send_ref):
    turned = dot3((across[0][...], across[1][...]), parts)
    place_modes(spectra_of(turned, depth), send_ref)


def taken_rows(recv_ref):
    rows = []
    for p in range(2):
        for g in range(2):
            for r in range(2):
                pieces = [recv_ref[pl.ds(kzh * 8 + r * 4 + p * 2 + g, 32, stride=16), :] for kzh in range(2)]
                rows.append(jnp.concatenate(pieces, 1))
    return split(jnp.concatenate(rows, 0))


def cells_from(recv_ref, back, depth):
    left = taken_rows(recv_ref)
    depth = [depth(k) for k in range(4)]
    even = dot3(left, (depth[0][...], depth[1][...]), dot_t)
    odd = dot3(left, (depth[2][...], depth[3][...]), dot_t)
    real, imag = even[:128] - odd[128:], odd[:128] + even[128:]
    rows = [jnp.concatenate([part[:64], part[64:]], 1) for part in (real, imag)]
    back = [back(k) for k in range(2)]
    return dot3((back[0][...], back[1][...]), split(jnp.concatenate(rows, 0)))


def plain_rows(field_ref, g):
    low_rows, high_rows = [], []
    lane = lax.broadcasted_iota(jnp.int32, (128, 128), 1) < 64
    for pair in range(8):
        first = field_ref[g * 16 + 2 * pair]
        second = field_ref[g * 16 + 2 * pair + 1]
        low_rows.append(jnp.where(lane, first, pltpu.roll(second, 64, 1)))
        high_rows.append(jnp.where(lane, pltpu.roll(first, 64, 1), second))
    return jnp.concatenate([jnp.concatenate(low_rows, 1), jnp.concatenate(high_rows, 1)], 0)


def lift_body(near, fetch, outs, put, scratch):
    across = (fetch(0)[...], fetch(1)[...])
    turned = [dot3(across, split(plain_rows(fetch(2 + g), 0))) for g in range(2)]
    place_modes(spectra_of(jnp.concatenate(turned, 1), [fetch(k) for k in range(4, 8)]), outs[0])


def point_chunks(parts_at, mix, bias, out_ref):
    for q in range(8):
        mixed = dot3(parts_at(q), mix) + bias
        out_ref[:, q * 128 : q * 128 + 128] = mixed[:, :128]
        out_ref[:, 1024 + q * 128 : 1152 + q * 128] = mixed[:, 128:]


def both(value, q):
    return jnp.concatenate([value[:, q * 128 : q * 128 + 128], value[:, 1024 + q * 128 : 1152 + q * 128]], 1)


def gelu_parts(x):
    square = x * x
    cubic = square * CUBE
    bend = jnp.tanh(x * (cubic + ROOT))
    above = bend + 1.0
    twice = x * above
    slope = above + (twice * (1.0 - bend)) * (cubic * 3.0 + ROOT)
    return twice, slope


def tiles(body, rows=16, lanes=512, height=256, width=2048):
    def step(index, carry):
        start = pl.multiple_of(index * rows, rows)
        for column in range(0, width, lanes):
            body(pl.ds(start, rows), slice(column, column + lanes))
        return carry

    lax.fori_loop(0, height // rows, step, 0)


def one_body(near, fetch, outs, put, scratch):
    send_ref, state_ref, slope_ref = outs
    pre, high, low = scratch
    pre[...] = cells_from(near[0], lambda k: fetch(4 + k), fetch)
    local_ref = fetch(6)

    def body(rows, columns):
        twice, slope = gelu_parts(pre[rows, columns] + local_ref[rows, columns])
        state = 0.5 * twice
        state_ref[rows, columns] = state
        slope_ref[rows, columns] = 0.5 * slope
        high[rows, columns], low[rows, columns] = split(state)

    tiles(body)
    send_modes((high[...], low[...]), [fetch(7), fetch(8)], [fetch(k) for k in range(4)], send_ref)


def two_body(near, fetch, outs, put, scratch):
    send_ref, back_ref = outs
    pre, high, low, hidden, slope_h, slope_l, sums, local_ref = scratch
    state_ref, mix, bias = fetch(6), (fetch(16)[...], fetch(17)[...]), fetch(18)[:1, :]
    point_chunks(lambda q: split(both(state_ref, q)), mix, bias, local_ref)
    pre[...] = cells_from(near[0], lambda k: fetch(4 + k), fetch)

    def body(rows, columns):
        twice, slope = gelu_parts(pre[rows, columns] + local_ref[rows, columns])
        pre[rows, columns] = 0.5 * slope
        high[rows, columns], low[rows, columns] = split(0.5 * twice)

    tiles(body)
    up_h, up_l, rows_ref, down_h, down_l, ones_ref, target_ref = [fetch(k) for k in range(9, 16)]

    def lanes_of(q):
        starts = (q * 128, 1024 + q * 128)
        return [pl.ds(start if isinstance(start, int) else pl.multiple_of(start, 128), 128) for start in starts]

    def rise(q, slot):
        first, second = lanes_of(q)
        left = tuple(jnp.concatenate([part[:, first], part[:, second]], 1) for part in (high, low))
        hidden[slot] = dot3(left, (up_h[...], up_l[...]))

    def bend(slot):
        for start in range(0, 256, 16):
            rows = slice(start, start + 16)
            total = jnp.zeros((16, 128), f32)
            for b in range(8):
                columns = slice(b * 128, b * 128 + 128)
                twice, slope = gelu_parts(hidden[slot, rows, columns] + rows_ref[0:16, columns])
                total = total + twice * rows_ref[16:32, columns]
                slope_h[slot, rows, columns], slope_l[slot, rows, columns] = split(slope)
            sums[slot, rows, :128], sums[slot, rows, 128:] = split(total)

    def fall(q, slot):
        first, second = lanes_of(q)
        reach = dot3((slope_h[slot], slope_l[slot]), (down_h[...], down_l[...]), dot_t)
        misfit = dot(sums[slot, :, :128], ones_ref[...]) + dot(sums[slot, :, 128:], ones_ref[...]) - target_ref[:, first]
        back_ref[:, first] = pre[:, first] * (misfit * reach[:, :128])
        back_ref[:, second] = pre[:, second] * (misfit * reach[:, 128:])

    rise(0, 0)
    rise(1, 1)
    bend(0)

    def turn(j, carry):
        for slot, q in ((1, 2 * j + 1), (0, 2 * j + 2)):
            rise(q + 1, 1 - slot)
            fall(q - 1, 1 - slot)
            bend(slot)
        return carry

    lax.fori_loop(0, 3, turn, 0)
    fall(6, 0)
    bend(1)
    fall(7, 1)
    put(1)
    send_modes(split(back_ref[...]), [fetch(7), fetch(8)], [fetch(k) for k in range(4)], send_ref)


def back_body(near, fetch, outs, put, scratch):
    pre, high, low, local_ref = scratch
    slope_ref, state_ref, mix = fetch(9), fetch(6), (fetch(10)[...], fetch(11)[...])
    point_chunks(lambda q: split(both(state_ref, q)), mix, 0.0, local_ref)
    pre[...] = cells_from(near[0], lambda k: fetch(4 + k), fetch)

    def body(rows, columns):
        back = slope_ref[rows, columns] * (pre[rows, columns] + local_ref[rows, columns])
        high[rows, columns], low[rows, columns] = split(back)

    tiles(body)
    send_modes((high[...], low[...]), [fetch(7), fetch(8)], [fetch(k) for k in range(4)], outs[0])


def depth_weight():
    lane = lax.broadcasted_iota(jnp.int32, (1, 128), 1)
    first = lax.rem(lax.axis_index("sp"), 2) * 128
    return jnp.where(lane + first < 16, 1.0, 2.0)


def mode_rows(recv_ref, first, factor, rows_ref):
    spectrum = dot3((first[0][...], first[1][...]), split(recv_ref[...]))
    if factor is not None:
        spectrum = spectrum * factor
    lane = lax.broadcasted_iota(jnp.int32, (64, 128), 1)
    for kz in range(8):
        first = spectrum[:64] if kz == 0 else pltpu.roll(spectrum[:64], 128 - 16 * kz, 1)
        second = spectrum[64:] if kz == 1 else pltpu.roll(spectrum[64:], (144 - 16 * kz) % 128, 1)
        joined = jnp.where(lane < 16, first, jnp.where(lane < 32, second, 0.0))
        rows_ref[pl.ds(kz, 64, stride=8), :] = joined


def selected(rows_ref, table):
    high, low = split(rows_ref[...])
    return dot(high, table[...]) + dot(low, table[...])


def send_cells(sums_ref, factor, first_back, send_ref):
    kz_lane = lax.broadcasted_iota(jnp.int32, (64, 128), 1) // 16
    packed = [jnp.zeros((64, 128), f32) for _ in range(2)]
    for kz in range(8):
        for g in range(2):
            packed[g] = jnp.where(kz_lane == kz, sums_ref[pl.ds(g * 512 + kz, 64, stride=8), :], packed[g])
    joined = jnp.concatenate(packed, 0)
    if factor is not None:
        joined = joined * factor
    send_ref[...] = dot3((first_back[0][...], first_back[1][...]), split(joined))


def mix_body(near, fetch, outs, put, scratch):
    send_ref, rows_ref = outs
    wide, sums, out = scratch
    mode_rows(near[0], [fetch(0), fetch(1)], None, rows_ref)
    put(1)
    wide[...] = selected(rows_ref, fetch(2))
    weight_ref = fetch(3)

    def step(kx, carry):
        real = pl.ds(pl.multiple_of(kx * 8, 8), 8)
        imag = pl.ds(pl.multiple_of(256 + kx * 8, 8), 8)
        total_real = jnp.zeros((8, 128), f32)
        total_imag = jnp.zeros((8, 128), f32)
        for b in range(8):
            columns = slice(b * 128, b * 128 + 128)
            fr, fi = wide[real, columns], wide[imag, columns]
            wr, wi = weight_ref[real, columns], weight_ref[imag, columns]
            total_real = total_real + (fr * wr - fi * wi)
            total_imag = total_imag + (fr * wi + fi * wr)
        sums[real, :] = total_real
        sums[imag, :] = total_imag
        return carry

    lax.fori_loop(0, 32, step, 0, unroll=4)
    mixed = selected(sums, fetch(4))
    out[:512, :] = mixed[:, :128]
    out[512:, :] = mixed[:, 128:]
    send_cells(out, depth_weight(), [fetch(5), fetch(6)], send_ref)


def adjoint_body(near, fetch, outs, put, scratch):
    send_ref, rows_ref = outs
    wide, high, low, out = scratch
    mode_rows(near[0], [fetch(0), fetch(1)], depth_weight(), rows_ref)
    put(1)
    wide[...] = selected(rows_ref, fetch(2))
    weight_ref = fetch(3)

    def step(kx, carry):
        real = pl.ds(pl.multiple_of(kx * 16, 16), 16)
        imag = pl.ds(pl.multiple_of(256 + kx * 16, 16), 16)
        br, bi = wide[real, :], wide[imag, :]
        for b in range(8):
            columns = slice(b * 128, b * 128 + 128)
            wr, wi = weight_ref[real, columns], weight_ref[imag, columns]
            high[real, columns], low[real, columns] = split(br * wr + bi * wi)
            high[imag, columns], low[imag, columns] = split(bi * wr - br * wi)
        return carry

    lax.fori_loop(0, 16, step, 0)
    table = fetch(4)[...]
    mixed = dot(high[...], table) + dot(low[...], table)
    out[:512, :] = mixed[:, :128]
    out[512:, :] = mixed[:, 128:]
    send_cells(out, None, [fetch(5), fetch(6)], send_ref)


def outer_products(forward_ref, back_ref, spread_ref, tile_ref, grad_ref, put, wide, narrow):
    wide[...] = selected(forward_ref, spread_ref)
    narrow[...] = selected(back_ref, tile_ref)

    def step(kx, carry):
        real = pl.ds(pl.multiple_of(kx * 8, 8), 8)
        imag = pl.ds(pl.multiple_of(256 + kx * 8, 8), 8)
        br, bi = narrow[real, :], narrow[imag, :]
        for b in range(8):
            columns = slice(b * 128, b * 128 + 128)
            fr, fi = wide[real, columns], wide[imag, columns]
            grad_ref[real, columns] = fr * br + fi * bi
            grad_ref[imag, columns] = fr * bi - fi * br
        return carry

    for part in range(4):
        lax.fori_loop(part * 8, part * 8 + 8, step, 0, unroll=4)
        put(0, pl.ds(part * 64, 64))
        put(0, pl.ds(256 + part * 64, 64))


def grad_body(near, fetch, outs, put, scratch):
    outer_products(fetch(0), fetch(1), fetch(2), fetch(3), outs[0], put, *scratch)


def last_body(near, fetch, outs, put, scratch):
    rows, wide, narrow = scratch
    mode_rows(near[0], [fetch(0), fetch(1)], depth_weight(), rows)
    outer_products(fetch(2), rows, fetch(3), fetch(4), outs[0], put, wide, narrow)


def table_body(near, fetch, outs, put, scratch):
    point_one, point_two, hidden_t, hidden_bias, output, bias_one, bias_two, channels, hidden, target, cells = [
        fetch(k) for k in range(11)
    ]
    two_h, two_l, back_h, back_l, up_h, up_l, down_h, down_l, rows_ref, bias_ref, target_ref, local_ref = outs
    one_h, one_l = scratch
    z_row = lax.broadcasted_iota(jnp.int32, (256, 1024), 0) // 16 % 8
    z_column = lax.broadcasted_iota(jnp.int32, (256, 1024), 1) // 16 % 8
    same = z_row == z_column

    def widen(left, right, mask, high, low):
        for part, out in zip(split(left), (high, low)):
            rows = dot(channels[...], part).astype(bf16)
            out[...] = jnp.where(mask, right(rows), 0.0).astype(bf16)

    square = same[:, :256]
    to_channels = lambda rows: dot_t(rows, channels[...])
    to_hidden = lambda rows: dot(rows, hidden[...])
    widen(point_one[...].T, to_channels, square, one_h, one_l)
    widen(point_two[...].T, to_channels, square, two_h, two_l)
    widen(point_two[...], to_channels, square, back_h, back_l)
    widen(hidden_t[...], to_hidden, same, up_h, up_l)
    widen(hidden_t[...] * (0.5 * output[...]), to_hidden, same, down_h, down_l)

    def exact(values, product):
        high, low = split(values)
        last = (values - high.astype(f32) - low.astype(f32)).astype(bf16)
        return product(high) + (product(low) + product(last))

    rows_ref[0:16, :] = exact(jnp.broadcast_to(hidden_bias[...], (16, 128)), to_hidden)
    rows_ref[16:32, :] = exact(jnp.broadcast_to(0.5 * output[...], (16, 128)), to_hidden)
    bias_ref[...] = exact(jnp.broadcast_to(bias_two[...], (8, 32)), to_channels)
    spread = exact(target[...], lambda part: dot(part, cells[...]))
    target_ref[:128, :] = spread[:, :1024]
    target_ref[128:, :] = spread[:, 1024:]
    for k in range(11):
        put(k)
    turned = []
    for g in range(2):
        high, low = split(plain_rows(fetch(11), g))
        turned.append((dot(high, fetch(12)[...]).astype(bf16), dot(low, fetch(12)[...]).astype(bf16)))
    parts = tuple(jnp.concatenate([turned[0][k], turned[1][k]], 1) for k in range(2))
    bias = exact(jnp.broadcast_to(bias_one[...], (8, 32)), to_channels)[:1]
    point_chunks(lambda q: tuple(both(part, q) for part in parts), (one_h[...], one_l[...]), bias, local_ref)
    put(11)


def shards(
    lifted_field,
    target_field,
    spectral_one,
    spectral_two,
    pointwise_one,
    layer_bias_one,
    pointwise_two,
    layer_bias_two,
    hidden_weight,
    hidden_bias,
    output_weight,
):
    across = tuple(map(jnp.asarray, two_parts(across_table())))
    across_back = tuple(map(jnp.asarray, two_parts(np.ascontiguousarray(across_table().T))))
    depth, depth_lifted = (
        tuple(jnp.asarray(part) for wave in depth_table(major) for part in two_parts(wave)) for major in (False, True)
    )
    first = tuple(map(jnp.asarray, two_parts(first_table())))
    first_back = tuple(map(jnp.asarray, two_parts(np.ascontiguousarray(first_table().T))))
    spread, tile, gather, gather_rows = map(jnp.asarray, selectors())
    channels, hidden, ones, cells = map(jnp.asarray, head_selectors())
    turn = jnp.asarray(turn_table())

    field = lifted_field.reshape(W, 2, 64, 128).transpose(0, 2, 1, 3).reshape(W, 128, 128)
    target = target_field.reshape(2, 64, 128).transpose(1, 0, 2).reshape(128, 128)
    weights_one = spectral_one.reshape(512, 1024)
    weights_two = spectral_two.reshape(512, 1024)
    def exchange(blocks):
        moved = lax.all_to_all(blocks.reshape(64, 8, 128), "sp", split_axis=0, concat_axis=0, tiled=True)
        return moved.reshape(512, 128)

    block, grid, wide = (512, 128), (256, 2048), (512, 1024)
    vm = pltpu.VMEM
    near_out = (block, f32, "near")
    far_out = lambda shape, kind=f32: (shape, kind, "far")
    work = [vm(grid, f32), vm(grid, bf16), vm(grid, bf16)]
    mix_work = [vm(wide, f32), vm(block, f32), vm((1024, 128), f32)]

    (send,) = run(
        lift_body, "lift", 2 * 10**9, (), (*across, field, field, *depth_lifted), [near_out], [],
        parts={2: (0, 16), 3: (16, 32)},
    )
    recv = exchange(send)
    row = lambda vector: vector.reshape(1, -1)
    made = run(
        table_body, "tables", 6 * 10**9, (),
        (
            pointwise_one, pointwise_two, hidden_weight.T, row(hidden_bias), row(output_weight),
            row(layer_bias_one), row(layer_bias_two), channels, hidden, target, cells, field, turn,
        ),
        [far_out((256, 256), bf16)] * 4 + [far_out((256, 1024), bf16)] * 4
        + [far_out((32, 1024)), far_out((8, 256)), far_out((256, 1024)), far_out(grid)],
        [vm((256, 256), bf16), vm((256, 256), bf16)],
    )
    mix_two, mix_back, up, down = made[0:2], made[2:4], made[4:6], made[6:8]
    hidden_rows, bias_two, target_wide, local_one = made[8:]
    send, modes_one = run(
        mix_body, "mix_one", 10**9, (recv,), (*first, spread, weights_one, gather, *first_back, bias_two),
        [near_out, far_out(block)], mix_work,
    )
    recv = exchange(send)
    send, state_one, slope_one = run(
        one_body, "grid_one", 5 * 10**9, (recv,), (*depth, *across_back, local_one, *across),
        [near_out, far_out(grid), far_out(grid)], work, managed=True,
    )
    recv = exchange(send)
    send, modes_two = run(
        mix_body, "mix_two", 10**9, (recv,), (*first, spread, weights_two, gather, *first_back),
        [near_out, far_out(block)], mix_work, managed=True,
    )
    recv = exchange(send)
    send, back_two = run(
        two_body, "grid_two", 15 * 10**9, (recv,),
        (*depth, *across_back, state_one, *across, *up, hidden_rows, *down, ones, target_wide, *mix_two, bias_two),
        [near_out, far_out(grid)],
        work + [vm((2, 256, 1024), f32), vm((2, 256, 1024), bf16), vm((2, 256, 1024), bf16), vm((2, 256, 256), bf16), vm(grid, f32)],
        managed=True,
    )
    recv = exchange(send)
    send, modes_back = run(
        adjoint_body, "adjoint", 10**9, (recv,), (*first, tile, weights_two, gather_rows, *first_back),
        [near_out, far_out(block)], [vm(block, f32), vm(wide, bf16), vm(wide, bf16), vm((1024, 128), f32)],
        managed=True,
    )
    recv = exchange(send)
    (gradient_two,) = run(
        grad_body, "grad_two", 10**9, (), (modes_two, modes_back, spread, tile), [far_out(wide)], [vm(wide, f32), vm(block, f32)]
    )
    (send,) = run(
        back_body, "grid_back", 5 * 10**9, (recv,), (*depth, *across_back, back_two, *across, slope_one, *mix_back), [near_out],
        work + [vm(grid, f32)], managed=True,
    )
    recv = exchange(send)
    (gradient_one,) = run(
        last_body, "grad_one", 10**9, (recv,), (*first, modes_one, spread, tile), [far_out(wide)],
        [vm(block, f32), vm(wide, f32), vm(block, f32)],
    )
    shape = (2, KX, 8, W * W)
    return (gradient_one.reshape(shape), gradient_two.reshape(shape))


def solution(mesh):
    in_specs = (
        P("batch", "sp", None),
        P("sp", "batch"),
        P(None, None, "sp", None),
        P(None, None, "sp", None),
        P(),
        P(),
        P(),
        P(),
        P(),
        P(),
        P(),
    )
    out_specs = (P("batch", None, "sp", None), P("batch", None, "sp", None))
    return jax.shard_map(shards, mesh=mesh, in_specs=in_specs, out_specs=out_specs, check_vma=False)
```

```python
import jax
import jax.numpy as jnp
import ml_dtypes
import numpy as np
from jax import lax
from jax.experimental import pallas as pl
from jax.experimental.pallas import tpu as pltpu
from jax.sharding import PartitionSpec as P

W = 32
H = 128
NX = 128
NY = 128
NZ = 64
KX = 32
KY = 32
KZ = 16

f32 = jnp.float32
bf16 = jnp.bfloat16
ROOT = 0.7978845608028654
CUBE = 0.044715 * ROOT


def centred(number, length):
    indices = np.arange(number)
    return np.where(indices < number // 2, indices, length - number + indices)


def two_parts(table):
    high = table.astype(ml_dtypes.bfloat16)
    low = (table - high.astype(np.float64)).astype(ml_dtypes.bfloat16)
    return high, low


def across_table():
    y = 2 * np.arange(64)[None, :] + np.arange(2)[:, None]
    angle = 2 * np.pi * (centred(KY, NY)[:, None, None] * y[None] % NY) / NY
    waves = np.stack([np.cos(angle), -np.sin(angle)])
    return np.einsum("skab,rt->srkabt", waves, np.eye(2)).reshape(128, 256)


def rotation(angle):
    cosine, sine = np.cos(angle), np.sin(angle)
    return np.stack([np.stack([cosine, -sine]), np.stack([sine, cosine])])


def depth_table(channel_major):
    angle = 2 * np.pi * (np.arange(NZ)[:, None] * np.arange(KZ)[None] % NZ) / NZ
    form = "zk,cd->czkd" if channel_major else "zk,cd->zckd"
    return [np.einsum(form, wave(angle), np.eye(16)).reshape(1024, 256) for wave in (np.cos, np.sin)]


def first_table():
    places = 2 * np.arange(64)[:, None] + np.arange(2)[None]
    angle = 2 * np.pi * (centred(KX, NX)[:, None, None] * places[None] % NX) / NX
    table = np.einsum("stkdr,gh->gtkdrsh", rotation(angle), np.eye(2))
    return table.reshape(128, 512) / 1024.0


def selectors():
    eye16, eye32 = np.eye(16), np.eye(32)
    lanes = np.zeros((128, 32))
    lanes[:32] = eye32
    spread = np.einsum("li,o->lio", lanes, np.ones(32)).reshape(128, 1024)
    tile = np.einsum("lo,i->lio", lanes, np.ones(4)).reshape(128, 128)
    halves = eye32.reshape(32, 2, 16)
    gather = np.einsum("i,ogc,k->iogkc", np.ones(4), halves, np.ones(8)).reshape(128, 256)
    gather_rows = np.einsum("igc,o,k->iogkc", halves, np.ones(32), np.ones(8)).reshape(1024, 256)
    return [part.astype(ml_dtypes.bfloat16) for part in (spread, tile, gather, gather_rows)]


def head_selectors():
    one = ml_dtypes.bfloat16
    channels = np.einsum("z,igc->gzci", np.ones(8), np.eye(32).reshape(32, 2, 16)).reshape(256, 32)
    hidden = np.einsum("hbu,z->hbzu", np.eye(128).reshape(128, 8, 16), np.ones(8)).reshape(128, 1024)
    ones = np.einsum("zy,uc->zuyc", np.eye(8), np.ones((16, 16))).reshape(128, 128)
    cells = np.einsum("ab,zy,c->bzayc", np.eye(2), np.eye(64), np.ones(16)).reshape(128, 2048)
    return channels.astype(one), hidden.astype(one), ones.astype(one), cells.astype(one)


def turn_table():
    return np.einsum("zy,cd->czyd", np.eye(64), np.eye(16)).reshape(1024, 1024).astype(ml_dtypes.bfloat16)


def split(values):
    high = values.astype(bf16)
    return high, (values - high.astype(f32)).astype(bf16)


def dot(left, right):
    return lax.dot_general(left, right, (((1,), (0,)), ((), ())), preferred_element_type=f32)


def dot_t(left, right):
    return lax.dot_general(left, right, (((1,), (1,)), ((), ())), preferred_element_type=f32)


def dot3(left, right, product=dot):
    return product(left[0], right[0]) + (product(left[1], right[0]) + product(left[0], right[1]))


def run(body, name, flops, near, far, outs, scratch, parts={}, managed=False, fetched=()):
    mine = list(fetched) if managed else list(range(len(far)))
    if managed:
        outs = [(shape, kind, "near") for shape, kind, _ in outs]
    leaving = [k for k, out in enumerate(outs) if out[2] == "far"]

    def kernel(*refs):
        refs = list(refs)
        take = lambda count: [refs.pop(0) for _ in range(count)]
        near_refs, far_refs, out_refs = take(len(near)), take(len(far)), take(len(outs))
        copied, filled = dict(zip(mine, take(len(mine)))), take(len(leaving))
        scratch_refs = take(len(scratch))
        arrived, left = refs
        for k, (start, stop) in parts.items():
            far_refs[k] = far_refs[k].at[pl.ds(start, stop - start)]
        copies = {k: pltpu.make_async_copy(far_refs[k], copied[k], arrived.at[k]) for k in mine}
        for copy in copies.values():
            copy.start()
        waited, started = set(), []

        def fetch(k):
            if k not in copies:
                return far_refs[k]
            if k not in waited:
                copies[k].wait()
                waited.add(k)
            return copied[k]

        def put(k, rows=None):
            if managed:
                return
            source, target = filled[leaving.index(k)], out_refs[k]
            if rows is not None:
                source, target = source.at[rows], target.at[rows]
            copy = pltpu.make_async_copy(source, target, left.at[len(started)])
            copy.start()
            started.append(copy)

        shown = [filled[leaving.index(k)] if k in leaving else out for k, out in enumerate(out_refs)]
        body(near_refs, fetch, shown, put, scratch_refs)
        for k in range(len(far)):
            fetch(k)
        for copy in started:
            copy.wait()

    far = [pltpu.with_memory_space_constraint(o, pltpu.HBM) if k in mine else o for k, o in enumerate(far)]
    vmem, hbm = pl.BlockSpec(memory_space=pltpu.VMEM), pl.BlockSpec(memory_space=pltpu.HBM)
    moved = sum(o.size * o.dtype.itemsize for o in (*near, *far))
    return pl.pallas_call(
        kernel,
        in_specs=[vmem] * len(near) + [hbm if k in mine else vmem for k in range(len(far))],
        out_specs=[hbm if out[2] == "far" else vmem for out in outs],
        out_shape=[pltpu.HBM(out[0], out[1]) if out[2] == "far" else jax.ShapeDtypeStruct(out[0], out[1]) for out in outs],
        scratch_shapes=[
            pltpu.VMEM((parts[k][1] - parts[k][0], *o.shape[1:]) if k in parts else o.shape, o.dtype)
            for k, o in enumerate(far)
            if k in mine
        ]
        + [pltpu.VMEM(outs[k][0], outs[k][1]) for k in leaving]
        + scratch
        + [pltpu.SemaphoreType.DMA((max(1, len(far)),)), pltpu.SemaphoreType.DMA((16,))],
        name=name,
        cost_estimate=pl.CostEstimate(flops=flops, bytes_accessed=int(moved), transcendentals=0),
        compiler_params=pltpu.CompilerParams(vmem_limit_bytes=28 * 1024 * 1024),
    )(*near, *far)


def spectra_of(turned, depth):
    rows = [turned[s * 64 : s * 64 + 64, g * 1024 : g * 1024 + 1024] for s in range(2) for g in range(2)]
    left = split(jnp.concatenate(rows, 0))
    even = dot3(left, (depth[0][...], depth[1][...]))
    odd = dot3(left, (depth[2][...], depth[3][...]))
    return even[:128] + odd[128:], even[128:] - odd[:128]


def place_modes(spectra, send_ref):
    for p in range(2):
        for g in range(2):
            for r in range(2):
                for kzh in range(2):
                    row = g * 64 + r * 32
                    send_ref[pl.ds(kzh * 8 + r * 4 + p * 2 + g, 32, stride=16), :] = spectra[p][
                        row : row + 32, kzh * 128 : kzh * 128 + 128
                    ]


def taken_rows(recv_ref):
    rows = []
    for p in range(2):
        for g in range(2):
            for r in range(2):
                pieces = [recv_ref[pl.ds(kzh * 8 + r * 4 + p * 2 + g, 32, stride=16), :] for kzh in range(2)]
                rows.append(jnp.concatenate(pieces, 1))
    return split(jnp.concatenate(rows, 0))


def deep_cells(recv_ref, depth, deep):
    left = taken_rows(recv_ref)
    even = dot3(left, (depth[0][...], depth[1][...]), dot_t)
    odd = dot3(left, (depth[2][...], depth[3][...]), dot_t)
    for p, part in enumerate((even[:128] - odd[128:], odd[:128] + even[128:])):
        for g in range(2):
            rows, lanes = slice(p * 64, p * 64 + 64), slice(g * 1024, g * 1024 + 1024)
            deep[0][rows, lanes], deep[1][rows, lanes] = split(part[g * 64 : g * 64 + 64])


def chunk(ref, q):
    return jnp.concatenate([ref[:, q * 128 : q * 128 + 128], ref[:, 1024 + q * 128 : 1152 + q * 128]], 1)


def store_chunk(ref, q, value):
    ref[:, q * 128 : q * 128 + 128] = value[:, :128]
    ref[:, 1024 + q * 128 : 1152 + q * 128] = value[:, 128:]


def strips(q):
    for start in range(0, 256, 16):
        for g in range(2):
            place = g * 1024 + q * 128
            yield slice(start, start + 16), slice(g * 128, g * 128 + 128), slice(place, place + 128)


def in_step(stages, count=8):
    for i in range(count + max(lag for _, lag in stages)):
        for stage, lag in stages:
            if 0 <= i - lag < count:
                stage(i - lag, (i - lag) % 2)


def plain_rows(field_ref, g):
    low_rows, high_rows = [], []
    lane = lax.broadcasted_iota(jnp.int32, (128, 128), 1) < 64
    for pair in range(8):
        first = field_ref[g * 16 + 2 * pair]
        second = field_ref[g * 16 + 2 * pair + 1]
        low_rows.append(jnp.where(lane, first, pltpu.roll(second, 64, 1)))
        high_rows.append(jnp.where(lane, pltpu.roll(first, 64, 1), second))
    return jnp.concatenate([jnp.concatenate(low_rows, 1), jnp.concatenate(high_rows, 1)], 0)


def lift_body(near, fetch, outs, put, scratch):
    across = (fetch(0)[...], fetch(1)[...])
    turned = [dot3(across, split(plain_rows(fetch(2 + g), 0))) for g in range(2)]
    place_modes(spectra_of(jnp.concatenate(turned, 1), [fetch(k) for k in range(4, 8)]), outs[0])


def point_chunks(parts_at, mix, bias, out_ref):
    for q in range(8):
        mixed = dot3(parts_at(q), mix) + bias
        out_ref[:, q * 128 : q * 128 + 128] = mixed[:, :128]
        out_ref[:, 1024 + q * 128 : 1152 + q * 128] = mixed[:, 128:]


def both(value, q):
    return jnp.concatenate([value[:, q * 128 : q * 128 + 128], value[:, 1024 + q * 128 : 1152 + q * 128]], 1)


def gelu_parts(x):
    square = x * x
    cubic = square * CUBE
    bend = jnp.tanh(x * (cubic + ROOT))
    above = bend + 1.0
    twice = x * above
    slope = above + (twice * (1.0 - bend)) * (cubic * 3.0 + ROOT)
    return twice, slope


def one_body(near, fetch, outs, put, scratch):
    send_ref, state_ref, slope_ref = outs
    pre, high, low, turned, *deep = scratch
    depth, back, across = [fetch(k) for k in range(4)], [fetch(4), fetch(5)], [fetch(7), fetch(8)]
    deep_cells(near[0], depth, deep)
    local_ref = fetch(6)

    def rise(q, slot):
        pre[slot] = dot3((back[0][...], back[1][...]), tuple(chunk(part, q) for part in deep))

    def bend(q, slot):
        for rows, here, there in strips(q):
            twice, slope = gelu_parts(pre[slot, rows, here] + local_ref[rows, there])
            state = 0.5 * twice
            state_ref[rows, there] = state
            slope_ref[rows, there] = 0.5 * slope
            high[slot, rows, here], low[slot, rows, here] = split(state)

    def fall(q, slot):
        store_chunk(turned, q, dot3((across[0][...], across[1][...]), (high[slot], low[slot])))

    in_step([(rise, 0), (fall, 2), (bend, 1)])
    place_modes(spectra_of(turned[...], depth), send_ref)


def two_body(near, fetch, outs, put, scratch):
    send_ref, back_ref = outs
    pre, high, low, turned, deep_h, deep_l, slopes, hidden, slope_h, slope_l, sums, back_h, back_l = scratch
    depth, back, across = [fetch(k) for k in range(4)], [fetch(4), fetch(5)], [fetch(7), fetch(8)]
    up_h, up_l, rows_ref, down_h, down_l, ones_ref, target_ref = [fetch(k) for k in range(9, 16)]
    state_ref, mix_h, mix_l, bias_ref = fetch(6), fetch(16), fetch(17), fetch(18)
    deep_cells(near[0], depth, (deep_h, deep_l))

    def rise(q, slot):
        cells = dot3((back[0][...], back[1][...]), (chunk(deep_h, q), chunk(deep_l, q)))
        local = dot3(split(chunk(state_ref, q)), (mix_h[...], mix_l[...]))
        pre[slot] = cells + (local + bias_ref[:1, :])

    def bend(q, slot):
        for rows, here, there in strips(q):
            twice, slope = gelu_parts(pre[slot, rows, here])
            slopes[rows, there] = 0.5 * slope
            high[slot, rows, here], low[slot, rows, here] = split(0.5 * twice)

    def reach(q, slot):
        hidden[slot] = dot3((high[slot], low[slot]), (up_h[...], up_l[...]))

    def bend_hidden(q, slot):
        for start in range(0, 256, 16):
            rows = slice(start, start + 16)
            total = jnp.zeros((16, 128), f32)
            for b in range(8):
                columns = slice(b * 128, b * 128 + 128)
                twice, slope = gelu_parts(hidden[slot, rows, columns] + rows_ref[0:16, columns])
                total = total + twice * rows_ref[16:32, columns]
                slope_h[slot, rows, columns], slope_l[slot, rows, columns] = split(slope)
            sums[slot, rows, :128], sums[slot, rows, 128:] = split(total)

    def withdraw(q, slot):
        reached = dot3((slope_h[slot], slope_l[slot]), (down_h[...], down_l[...]), dot_t)
        misfit = dot(sums[slot, :, :128], ones_ref[...]) + dot(sums[slot, :, 128:], ones_ref[...])
        misfit = misfit - target_ref[:, q * 128 : q * 128 + 128]
        value = chunk(slopes, q) * (jnp.concatenate([misfit, misfit], 1) * reached)
        store_chunk(back_ref, q, value)
        back_h[slot], back_l[slot] = split(value)

    def fall(q, slot):
        store_chunk(turned, q, dot3((across[0][...], across[1][...]), (back_h[slot], back_l[slot])))

    in_step([(rise, 0), (reach, 2), (withdraw, 4), (fall, 5), (bend, 1), (bend_hidden, 3)])
    place_modes(spectra_of(turned[...], depth), send_ref)


def back_body(near, fetch, outs, put, scratch):
    pre, high, low, turned, *deep = scratch
    depth, back, across = [fetch(k) for k in range(4)], [fetch(4), fetch(5)], [fetch(7), fetch(8)]
    state_ref, slope_ref, mix_h, mix_l = fetch(6), fetch(9), fetch(10), fetch(11)
    deep_cells(near[0], depth, deep)

    def rise(q, slot):
        cells = dot3((back[0][...], back[1][...]), tuple(chunk(part, q) for part in deep))
        pre[slot] = cells + dot3(split(chunk(state_ref, q)), (mix_h[...], mix_l[...]))

    def bend(q, slot):
        for rows, here, there in strips(q):
            high[slot, rows, here], low[slot, rows, here] = split(slope_ref[rows, there] * pre[slot, rows, here])

    def fall(q, slot):
        store_chunk(turned, q, dot3((across[0][...], across[1][...]), (high[slot], low[slot])))

    in_step([(rise, 0), (fall, 2), (bend, 1)])
    place_modes(spectra_of(turned[...], depth), outs[0])


def depth_weight():
    lane = lax.broadcasted_iota(jnp.int32, (1, 128), 1)
    first = lax.rem(lax.axis_index("sp"), 2) * 128
    return jnp.where(lane + first < 16, 1.0, 2.0)


def mode_rows(recv_ref, first, factor, rows_ref):
    spectrum = dot3((first[0][...], first[1][...]), split(recv_ref[...]))
    if factor is not None:
        spectrum = spectrum * factor
    lane = lax.broadcasted_iota(jnp.int32, (64, 128), 1)
    for kz in range(8):
        first = spectrum[:64] if kz == 0 else pltpu.roll(spectrum[:64], 128 - 16 * kz, 1)
        second = spectrum[64:] if kz == 1 else pltpu.roll(spectrum[64:], (144 - 16 * kz) % 128, 1)
        joined = jnp.where(lane < 16, first, jnp.where(lane < 32, second, 0.0))
        rows_ref[pl.ds(kz, 64, stride=8), :] = joined


def selected(rows, table):
    high, low = split(rows)
    return dot(high, table[...]) + dot(low, table[...])


def mode_parts(part):
    return [slice(start + part * 64, start + part * 64 + 64) for start in (0, 256)]


def mode_tiles(part, rows):
    for start in range(part * 64, part * 64 + 64, rows):
        yield slice(start, start + rows), slice(256 + start, 256 + start + rows)


def widen_modes(rows_ref, table, wide):
    def stage(part, slot):
        for rows in mode_parts(part):
            wide[rows, :] = selected(rows_ref[rows, :], table)

    return stage


def send_cells(sums_ref, factor, first_back, send_ref):
    kz_lane = lax.broadcasted_iota(jnp.int32, (64, 128), 1) // 16
    packed = [jnp.zeros((64, 128), f32) for _ in range(2)]
    for kz in range(8):
        for g in range(2):
            packed[g] = jnp.where(kz_lane == kz, sums_ref[pl.ds(g * 512 + kz, 64, stride=8), :], packed[g])
    joined = jnp.concatenate(packed, 0)
    if factor is not None:
        joined = joined * factor
    send_ref[...] = dot3((first_back[0][...], first_back[1][...]), split(joined))


def mix_body(near, fetch, outs, put, scratch):
    send_ref, rows_ref = outs
    wide, sums, out = scratch
    mode_rows(near[0], [fetch(0), fetch(1)], None, rows_ref)
    put(1)
    spread, weight_ref, gather = fetch(2), fetch(3), fetch(4)

    def multiply(part, slot):
        for real, imag in mode_tiles(part, 8):
            total_real = jnp.zeros((8, 128), f32)
            total_imag = jnp.zeros((8, 128), f32)
            for b in range(8):
                columns = slice(b * 128, b * 128 + 128)
                fr, fi = wide[real, columns], wide[imag, columns]
                wr, wi = weight_ref[real, columns], weight_ref[imag, columns]
                total_real = total_real + (fr * wr - fi * wi)
                total_imag = total_imag + (fr * wi + fi * wr)
            sums[real, :] = total_real
            sums[imag, :] = total_imag

    def collect(part, slot):
        for rows in mode_parts(part):
            mixed = selected(sums[rows, :], gather)
            out[rows, :] = mixed[:, :128]
            out[512 + rows.start : 512 + rows.stop, :] = mixed[:, 128:]

    in_step([(widen_modes(rows_ref, spread, wide), 0), (collect, 2), (multiply, 1)], 4)
    send_cells(out, depth_weight(), [fetch(5), fetch(6)], send_ref)


def adjoint_body(near, fetch, outs, put, scratch):
    send_ref, rows_ref = outs
    wide, high, low, out = scratch
    mode_rows(near[0], [fetch(0), fetch(1)], depth_weight(), rows_ref)
    put(1)
    wide[...] = selected(rows_ref[...], fetch(2))
    weight_ref, gather = fetch(3), fetch(4)

    def multiply(part, slot):
        for real, imag in mode_tiles(part, 16):
            br, bi = wide[real, :], wide[imag, :]
            for b in range(8):
                columns = slice(b * 128, b * 128 + 128)
                wr, wi = weight_ref[real, columns], weight_ref[imag, columns]
                high[real, columns], low[real, columns] = split(br * wr + bi * wi)
                high[imag, columns], low[imag, columns] = split(bi * wr - br * wi)

    def collect(part, slot):
        for rows in mode_parts(part):
            mixed = dot(high[rows, :], gather[...]) + dot(low[rows, :], gather[...])
            out[rows, :] = mixed[:, :128]
            out[512 + rows.start : 512 + rows.stop, :] = mixed[:, 128:]

    in_step([(collect, 1), (multiply, 0)], 4)
    send_cells(out, None, [fetch(5), fetch(6)], send_ref)


def outer_products(forward_ref, back_ref, spread_ref, tile_ref, grad_ref, put, wide, narrow):
    narrow[...] = selected(back_ref[...], tile_ref)

    def multiply(part, slot):
        for real, imag in mode_tiles(part, 8):
            br, bi = narrow[real, :], narrow[imag, :]
            for b in range(8):
                columns = slice(b * 128, b * 128 + 128)
                fr, fi = wide[real, columns], wide[imag, columns]
                grad_ref[real, columns] = fr * br + fi * bi
                grad_ref[imag, columns] = fr * bi - fi * br
        for rows in mode_parts(part):
            put(0, pl.ds(rows.start, 64))

    in_step([(widen_modes(forward_ref, spread_ref, wide), 0), (multiply, 1)], 4)


def grad_body(near, fetch, outs, put, scratch):
    outer_products(fetch(0), fetch(1), fetch(2), fetch(3), outs[0], put, *scratch)


def last_body(near, fetch, outs, put, scratch):
    rows, wide, narrow = scratch
    mode_rows(near[0], [fetch(0), fetch(1)], depth_weight(), rows)
    outer_products(fetch(2), rows, fetch(3), fetch(4), outs[0], put, wide, narrow)


def table_body(near, fetch, outs, put, scratch):
    point_one, point_two, hidden_t, hidden_bias, output, bias_one, bias_two, channels, hidden, target, cells = [
        fetch(k) for k in range(11)
    ]
    two_h, two_l, back_h, back_l, up_h, up_l, down_h, down_l, rows_ref, bias_ref, target_ref, local_ref = outs
    one_h, one_l = scratch
    z_row = lax.broadcasted_iota(jnp.int32, (256, 1024), 0) // 16 % 8
    z_column = lax.broadcasted_iota(jnp.int32, (256, 1024), 1) // 16 % 8
    same = z_row == z_column

    def widen(left, right, mask, high, low):
        for part, out in zip(split(left), (high, low)):
            rows = dot(channels[...], part).astype(bf16)
            out[...] = jnp.where(mask, right(rows), 0.0).astype(bf16)

    square = same[:, :256]
    to_channels = lambda rows: dot_t(rows, channels[...])
    to_hidden = lambda rows: dot(rows, hidden[...])
    widen(point_one[...].T, to_channels, square, one_h, one_l)
    widen(point_two[...].T, to_channels, square, two_h, two_l)
    widen(point_two[...], to_channels, square, back_h, back_l)
    widen(hidden_t[...], to_hidden, same, up_h, up_l)
    widen(hidden_t[...] * (0.5 * output[...]), to_hidden, same, down_h, down_l)

    def exact(values, product):
        high, low = split(values)
        last = (values - high.astype(f32) - low.astype(f32)).astype(bf16)
        return product(high) + (product(low) + product(last))

    rows_ref[0:16, :] = exact(jnp.broadcast_to(hidden_bias[...], (16, 128)), to_hidden)
    rows_ref[16:32, :] = exact(jnp.broadcast_to(0.5 * output[...], (16, 128)), to_hidden)
    bias_ref[...] = exact(jnp.broadcast_to(bias_two[...], (8, 32)), to_channels)
    spread = exact(target[...], lambda part: dot(part, cells[...]))
    target_ref[:128, :] = spread[:, :1024]
    target_ref[128:, :] = spread[:, 1024:]
    for k in range(11):
        put(k)
    turned = []
    for g in range(2):
        high, low = split(plain_rows(fetch(11), g))
        turned.append((dot(high, fetch(12)[...]).astype(bf16), dot(low, fetch(12)[...]).astype(bf16)))
    parts = tuple(jnp.concatenate([turned[0][k], turned[1][k]], 1) for k in range(2))
    bias = exact(jnp.broadcast_to(bias_one[...], (8, 32)), to_channels)[:1]
    point_chunks(lambda q: tuple(both(part, q) for part in parts), (one_h[...], one_l[...]), bias, local_ref)
    put(11)


def shards(
    lifted_field,
    target_field,
    spectral_one,
    spectral_two,
    pointwise_one,
    layer_bias_one,
    pointwise_two,
    layer_bias_two,
    hidden_weight,
    hidden_bias,
    output_weight,
):
    across = tuple(map(jnp.asarray, two_parts(across_table())))
    across_back = tuple(map(jnp.asarray, two_parts(np.ascontiguousarray(across_table().T))))
    depth, depth_lifted = (
        tuple(jnp.asarray(part) for wave in depth_table(major) for part in two_parts(wave)) for major in (False, True)
    )
    first = tuple(map(jnp.asarray, two_parts(first_table())))
    first_back = tuple(map(jnp.asarray, two_parts(np.ascontiguousarray(first_table().T))))
    spread, tile, gather, gather_rows = map(jnp.asarray, selectors())
    channels, hidden, ones, cells = map(jnp.asarray, head_selectors())
    turn = jnp.asarray(turn_table())

    field = lifted_field.reshape(W, 2, 64, 128).transpose(0, 2, 1, 3).reshape(W, 128, 128)
    target = target_field.reshape(2, 64, 128).transpose(1, 0, 2).reshape(128, 128)
    weights_one = spectral_one.reshape(512, 1024)
    weights_two = spectral_two.reshape(512, 1024)
    def exchange(blocks):
        moved = lax.all_to_all(blocks.reshape(64, 8, 128), "sp", split_axis=0, concat_axis=0, tiled=True)
        return moved.reshape(512, 128)

    block, grid, wide = (512, 128), (256, 2048), (512, 1024)
    vm = pltpu.VMEM
    near_out = (block, f32, "near")
    far_out = lambda shape, kind=f32: (shape, kind, "far")
    pair = lambda lanes, kind: vm((2, 256, lanes), kind)
    work = [pair(256, f32), pair(256, bf16), pair(256, bf16), vm((128, 2048), f32), vm((128, 2048), bf16), vm((128, 2048), bf16)]
    mix_work = [vm(wide, f32), vm(block, f32), vm((1024, 128), f32)]

    (send,) = run(
        lift_body, "lift", 2 * 10**9, (), (*across, field, field, *depth_lifted), [near_out], [],
        parts={2: (0, 16), 3: (16, 32)},
    )
    recv = exchange(send)
    row = lambda vector: vector.reshape(1, -1)
    made = run(
        table_body, "tables", 6 * 10**9, (),
        (
            pointwise_one, pointwise_two, hidden_weight.T, row(hidden_bias), row(output_weight),
            row(layer_bias_one), row(layer_bias_two), channels, hidden, target, cells, field, turn,
        ),
        [far_out((256, 256), bf16)] * 4 + [far_out((256, 1024), bf16)] * 4
        + [far_out((32, 1024)), far_out((8, 256)), far_out((256, 1024)), far_out(grid)],
        [vm((256, 256), bf16), vm((256, 256), bf16)],
    )
    mix_two, mix_back, up, down = made[0:2], made[2:4], made[4:6], made[6:8]
    hidden_rows, bias_two, target_wide, local_one = made[8:]
    send, modes_one = run(
        mix_body, "mix_one", 10**9, (recv,), (*first, spread, weights_one, gather, *first_back, bias_two),
        [near_out, far_out(block)], mix_work,
    )
    recv = exchange(send)
    send, state_one, slope_one = run(
        one_body, "grid_one", 5 * 10**9, (recv,), (*depth, *across_back, local_one, *across),
        [near_out, far_out(grid), far_out(grid)], work, managed=True, fetched=(6,),
    )
    recv = exchange(send)
    send, modes_two = run(
        mix_body, "mix_two", 10**9, (recv,), (*first, spread, weights_two, gather, *first_back),
        [near_out, far_out(block)], mix_work, managed=True,
    )
    recv = exchange(send)
    send, back_two = run(
        two_body, "grid_two", 15 * 10**9, (recv,),
        (*depth, *across_back, state_one, *across, *up, hidden_rows, *down, ones, target_wide, *mix_two, bias_two),
        [near_out, far_out(grid)],
        work
        + [vm(grid, f32), pair(1024, f32), pair(1024, bf16), pair(1024, bf16), pair(256, bf16), pair(256, bf16), pair(256, bf16)],
        managed=True,
    )
    recv = exchange(send)
    send, modes_back = run(
        adjoint_body, "adjoint", 10**9, (recv,), (*first, tile, weights_two, gather_rows, *first_back),
        [near_out, far_out(block)], [vm(block, f32), vm(wide, bf16), vm(wide, bf16), vm((1024, 128), f32)],
        managed=True,
    )
    recv = exchange(send)
    (gradient_two,) = run(
        grad_body, "grad_two", 10**9, (), (modes_two, modes_back, spread, tile), [far_out(wide)], [vm(wide, f32), vm(block, f32)]
    )
    (send,) = run(
        back_body, "grid_back", 5 * 10**9, (recv,), (*depth, *across_back, back_two, *across, slope_one, *mix_back), [near_out], work, managed=True,
    )
    recv = exchange(send)
    (gradient_one,) = run(
        last_body, "grad_one", 10**9, (recv,), (*first, modes_one, spread, tile), [far_out(wide)],
        [vm(block, f32), vm(wide, f32), vm(block, f32)],
    )
    shape = (2, KX, 8, W * W)
    return (gradient_one.reshape(shape), gradient_two.reshape(shape))


def solution(mesh):
    in_specs = (
        P("batch", "sp", None),
        P("sp", "batch"),
        P(None, None, "sp", None),
        P(None, None, "sp", None),
        P(),
        P(),
        P(),
        P(),
        P(),
        P(),
        P(),
    )
    out_specs = (P("batch", None, "sp", None), P("batch", None, "sp", None))
    return jax.shard_map(shards, mesh=mesh, in_specs=in_specs, out_specs=out_specs, check_vma=False)
```

```python
import jax
import jax.numpy as jnp
import ml_dtypes
import numpy as np
from jax import lax
from jax.experimental import pallas as pl
from jax.experimental.pallas import tpu as pltpu
from jax.sharding import PartitionSpec as P

W = 32
H = 128
NX = 128
NY = 128
NZ = 64
KX = 32
KY = 32
KZ = 16

f32 = jnp.float32
bf16 = jnp.bfloat16
ROOT = 0.7978845608028654
CUBE = 0.044715 * ROOT


def centred(number, length):
    indices = np.arange(number)
    return np.where(indices < number // 2, indices, length - number + indices)


def two_parts(table):
    high = table.astype(ml_dtypes.bfloat16)
    low = (table - high.astype(np.float64)).astype(ml_dtypes.bfloat16)
    return high, low


def across_table():
    y = 2 * np.arange(64)[None, :] + np.arange(2)[:, None]
    angle = 2 * np.pi * (centred(KY, NY)[:, None, None] * y[None] % NY) / NY
    waves = np.stack([np.cos(angle), -np.sin(angle)])
    return np.einsum("skab,rt->srkabt", waves, np.eye(2)).reshape(128, 256)


def rotation(angle):
    cosine, sine = np.cos(angle), np.sin(angle)
    return np.stack([np.stack([cosine, -sine]), np.stack([sine, cosine])])


def depth_table(channel_major):
    angle = 2 * np.pi * (np.arange(NZ)[:, None] * np.arange(KZ)[None] % NZ) / NZ
    form = "zk,cd->czkd" if channel_major else "zk,cd->zckd"
    return [np.einsum(form, wave(angle), np.eye(16)).reshape(1024, 256) for wave in (np.cos, np.sin)]


def first_table():
    places = 2 * np.arange(64)[:, None] + np.arange(2)[None]
    angle = 2 * np.pi * (centred(KX, NX)[:, None, None] * places[None] % NX) / NX
    table = np.einsum("stkdr,gh->gtkdrsh", rotation(angle), np.eye(2))
    return table.reshape(128, 512) / 1024.0


def selectors():
    eye16, eye32 = np.eye(16), np.eye(32)
    lanes = np.zeros((128, 32))
    lanes[:32] = eye32
    spread = np.einsum("li,o->lio", lanes, np.ones(32)).reshape(128, 1024)
    tile = np.einsum("lo,i->lio", lanes, np.ones(4)).reshape(128, 128)
    halves = eye32.reshape(32, 2, 16)
    gather = np.einsum("i,ogc,k->iogkc", np.ones(4), halves, np.ones(8)).reshape(128, 256)
    gather_rows = np.einsum("igc,o,k->iogkc", halves, np.ones(32), np.ones(8)).reshape(1024, 256)
    return [part.astype(ml_dtypes.bfloat16) for part in (spread, tile, gather, gather_rows)]


def head_selectors():
    one = ml_dtypes.bfloat16
    channels = np.einsum("z,igc->gzci", np.ones(8), np.eye(32).reshape(32, 2, 16)).reshape(256, 32)
    hidden = np.einsum("hbu,z->hbzu", np.eye(128).reshape(128, 8, 16), np.ones(8)).reshape(128, 1024)
    ones = np.einsum("zy,uc->zuyc", np.eye(8), np.ones((16, 16))).reshape(128, 128)
    cells = np.einsum("ab,zy,c->bzayc", np.eye(2), np.eye(64), np.ones(16)).reshape(128, 2048)
    return channels.astype(one), hidden.astype(one), ones.astype(one), cells.astype(one)


def turn_table():
    return np.einsum("zy,cd->czyd", np.eye(64), np.eye(16)).reshape(1024, 1024).astype(ml_dtypes.bfloat16)


def split(values):
    high = values.astype(bf16)
    return high, (values - high.astype(f32)).astype(bf16)


def dot(left, right):
    return lax.dot_general(left, right, (((1,), (0,)), ((), ())), preferred_element_type=f32)


def dot_t(left, right):
    return lax.dot_general(left, right, (((1,), (1,)), ((), ())), preferred_element_type=f32)


def dot3(left, right, product=dot):
    return product(left[0], right[0]) + (product(left[1], right[0]) + product(left[0], right[1]))


def run(body, name, flops, near, far, outs, scratch, parts={}, managed=False, fetched=()):
    mine = list(fetched) if managed else list(range(len(far)))
    if managed:
        outs = [(shape, kind, "near" if place == "far" else place) for shape, kind, place in outs]
    leaving = [k for k, out in enumerate(outs) if out[2] != "near"]

    def kernel(*refs):
        refs = list(refs)
        take = lambda count: [refs.pop(0) for _ in range(count)]
        near_refs, far_refs, out_refs = take(len(near)), take(len(far)), take(len(outs))
        copied, filled = dict(zip(mine, take(len(mine)))), take(len(leaving))
        scratch_refs = take(len(scratch))
        arrived, left = refs
        for k, (start, stop) in parts.items():
            far_refs[k] = far_refs[k].at[pl.ds(start, stop - start)]
        copies = {k: pltpu.make_async_copy(far_refs[k], copied[k], arrived.at[k]) for k in mine}
        for copy in copies.values():
            copy.start()
        waited, started = set(), []

        def fetch(k):
            if k not in copies:
                return far_refs[k]
            if k not in waited:
                copies[k].wait()
                waited.add(k)
            return copied[k]

        def put(k, rows=None):
            if k not in leaving:
                return
            source, target = filled[leaving.index(k)], out_refs[k]
            if rows is not None:
                source, target = source.at[rows], target.at[rows]
            copy = pltpu.make_async_copy(source, target, left.at[len(started)])
            copy.start()
            started.append(copy)

        shown = [filled[leaving.index(k)] if k in leaving else out for k, out in enumerate(out_refs)]
        body(near_refs, fetch, shown, put, scratch_refs)
        for k in range(len(far)):
            fetch(k)
        for copy in started:
            copy.wait()

    far = [pltpu.with_memory_space_constraint(o, pltpu.HBM) if k in mine else o for k, o in enumerate(far)]
    vmem, hbm = pl.BlockSpec(memory_space=pltpu.VMEM), pl.BlockSpec(memory_space=pltpu.HBM)
    moved = sum(o.size * o.dtype.itemsize for o in (*near, *far))
    return pl.pallas_call(
        kernel,
        in_specs=[vmem] * len(near) + [hbm if k in mine else vmem for k in range(len(far))],
        out_specs=[vmem if out[2] == "near" else hbm for out in outs],
        out_shape=[jax.ShapeDtypeStruct(out[0], out[1]) if out[2] == "near" else pltpu.HBM(out[0], out[1]) for out in outs],
        scratch_shapes=[
            pltpu.VMEM((parts[k][1] - parts[k][0], *o.shape[1:]) if k in parts else o.shape, o.dtype)
            for k, o in enumerate(far)
            if k in mine
        ]
        + [pltpu.VMEM(outs[k][0], outs[k][1]) for k in leaving]
        + scratch
        + [pltpu.SemaphoreType.DMA((max(1, len(far)),)), pltpu.SemaphoreType.DMA((16,))],
        name=name,
        cost_estimate=pl.CostEstimate(flops=flops, bytes_accessed=int(moved), transcendentals=0),
        compiler_params=pltpu.CompilerParams(vmem_limit_bytes=28 * 1024 * 1024),
    )(*near, *far)


def spectra_of(turned, depth):
    rows = [turned[s * 64 : s * 64 + 64, g * 1024 : g * 1024 + 1024] for s in range(2) for g in range(2)]
    left = split(jnp.concatenate(rows, 0))
    even = dot3(left, (depth[0][...], depth[1][...]))
    odd = dot3(left, (depth[2][...], depth[3][...]))
    return even[:128] + odd[128:], even[128:] - odd[:128]


def place_modes(spectra, send_ref):
    for p in range(2):
        for g in range(2):
            for r in range(2):
                for kzh in range(2):
                    row = g * 64 + r * 32
                    send_ref[pl.ds(kzh * 8 + r * 4 + p * 2 + g, 32, stride=16), :] = spectra[p][
                        row : row + 32, kzh * 128 : kzh * 128 + 128
                    ]


def taken_rows(recv_ref):
    rows = []
    for p in range(2):
        for g in range(2):
            for r in range(2):
                pieces = [recv_ref[pl.ds(kzh * 8 + r * 4 + p * 2 + g, 32, stride=16), :] for kzh in range(2)]
                rows.append(jnp.concatenate(pieces, 1))
    return split(jnp.concatenate(rows, 0))


def deep_cells(recv_ref, depth, deep):
    left = taken_rows(recv_ref)
    even = dot3(left, (depth[0][...], depth[1][...]), dot_t)
    odd = dot3(left, (depth[2][...], depth[3][...]), dot_t)
    for p, part in enumerate((even[:128] - odd[128:], odd[:128] + even[128:])):
        for g in range(2):
            rows, lanes = slice(p * 64, p * 64 + 64), slice(g * 1024, g * 1024 + 1024)
            deep[0][rows, lanes], deep[1][rows, lanes] = split(part[g * 64 : g * 64 + 64])


def chunk(ref, q):
    return jnp.concatenate([ref[:, q * 128 : q * 128 + 128], ref[:, 1024 + q * 128 : 1152 + q * 128]], 1)


def store_chunk(ref, q, value):
    ref[:, q * 128 : q * 128 + 128] = value[:, :128]
    ref[:, 1024 + q * 128 : 1152 + q * 128] = value[:, 128:]


def strips(q):
    for start in range(0, 256, 16):
        for g in range(2):
            place = g * 1024 + q * 128
            yield slice(start, start + 16), slice(g * 128, g * 128 + 128), slice(place, place + 128)


def in_step(stages, count=8):
    for i in range(count + max(lag for _, lag in stages)):
        for stage, lag in stages:
            if 0 <= i - lag < count:
                stage(i - lag, (i - lag) % 2)


def plain_rows(field_ref, start, pairs):
    low_rows, high_rows = [], []
    lane = lax.broadcasted_iota(jnp.int32, (128, 128), 1) < 64
    for pair in range(pairs):
        first = field_ref[start + 2 * pair]
        second = field_ref[start + 2 * pair + 1]
        low_rows.append(jnp.where(lane, first, pltpu.roll(second, 64, 1)))
        high_rows.append(jnp.where(lane, pltpu.roll(first, 64, 1), second))
    return jnp.concatenate([jnp.concatenate(low_rows, 1), jnp.concatenate(high_rows, 1)], 0)


def lift_body(near, fetch, outs, put, scratch):
    across = (fetch(0)[...], fetch(1)[...])
    turned = [dot3(across, split(plain_rows(fetch(2 + part), 0, 4))) for part in range(4)]
    place_modes(spectra_of(jnp.concatenate(turned, 1), [fetch(k) for k in range(6, 10)]), outs[0])


def point_chunks(parts_at, mix, bias, out_ref):
    for q in range(8):
        mixed = dot3(parts_at(q), mix) + bias
        out_ref[:, q * 128 : q * 128 + 128] = mixed[:, :128]
        out_ref[:, 1024 + q * 128 : 1152 + q * 128] = mixed[:, 128:]


def both(value, q):
    return jnp.concatenate([value[:, q * 128 : q * 128 + 128], value[:, 1024 + q * 128 : 1152 + q * 128]], 1)


def gelu_parts(x):
    square = x * x
    cubic = square * CUBE
    bend = jnp.tanh(x * (cubic + ROOT))
    above = bend + 1.0
    twice = x * above
    slope = above + (twice * (1.0 - bend)) * (cubic * 3.0 + ROOT)
    return twice, slope


def one_body(near, fetch, outs, put, scratch):
    send_ref, state_ref, slope_ref = outs
    pre, high, low, turned, *deep = scratch
    depth, back, across = [fetch(k) for k in range(4)], [fetch(4), fetch(5)], [fetch(7), fetch(8)]
    deep_cells(near[0], depth, deep)
    local_ref = fetch(6)

    def rise(q, slot):
        pre[slot] = dot3((back[0][...], back[1][...]), tuple(chunk(part, q) for part in deep))

    def bend(q, slot):
        for rows, here, there in strips(q):
            twice, slope = gelu_parts(pre[slot, rows, here] + local_ref[rows, there])
            state = 0.5 * twice
            state_ref[rows, there] = state
            slope_ref[rows, there] = 0.5 * slope
            high[slot, rows, here], low[slot, rows, here] = split(state)

    def fall(q, slot):
        store_chunk(turned, q, dot3((across[0][...], across[1][...]), (high[slot], low[slot])))

    in_step([(rise, 0), (fall, 2), (bend, 1)])
    place_modes(spectra_of(turned[...], depth), send_ref)


def two_body(near, fetch, outs, put, scratch):
    send_ref, back_ref = outs
    pre, high, low, turned, deep_h, deep_l, slopes, hidden, slope_h, slope_l, sums, back_h, back_l = scratch
    depth, back, across = [fetch(k) for k in range(4)], [fetch(4), fetch(5)], [fetch(7), fetch(8)]
    up_h, up_l, rows_ref, down_h, down_l, ones_ref, target_ref = [fetch(k) for k in range(9, 16)]
    state_ref, mix_h, mix_l, bias_ref = fetch(6), fetch(16), fetch(17), fetch(18)
    deep_cells(near[0], depth, (deep_h, deep_l))

    def rise(q, slot):
        cells = dot3((back[0][...], back[1][...]), (chunk(deep_h, q), chunk(deep_l, q)))
        local = dot3(split(chunk(state_ref, q)), (mix_h[...], mix_l[...]))
        pre[slot] = cells + (local + bias_ref[:1, :])

    def bend(q, slot):
        for rows, here, there in strips(q):
            twice, slope = gelu_parts(pre[slot, rows, here])
            slopes[rows, there] = 0.5 * slope
            high[slot, rows, here], low[slot, rows, here] = split(0.5 * twice)

    def reach(q, slot):
        hidden[slot] = dot3((high[slot], low[slot]), (up_h[...], up_l[...]))

    def bend_hidden(q, slot):
        for start in range(0, 256, 16):
            rows = slice(start, start + 16)
            total = jnp.zeros((16, 128), f32)
            for b in range(8):
                columns = slice(b * 128, b * 128 + 128)
                twice, slope = gelu_parts(hidden[slot, rows, columns] + rows_ref[0:16, columns])
                total = total + twice * rows_ref[16:32, columns]
                slope_h[slot, rows, columns], slope_l[slot, rows, columns] = split(slope)
            sums[slot, rows, :128], sums[slot, rows, 128:] = split(total)

    def withdraw(q, slot):
        reached = dot3((slope_h[slot], slope_l[slot]), (down_h[...], down_l[...]), dot_t)
        misfit = dot(sums[slot, :, :128], ones_ref[...]) + dot(sums[slot, :, 128:], ones_ref[...])
        misfit = misfit - target_ref[:, q * 128 : q * 128 + 128]
        value = chunk(slopes, q) * (jnp.concatenate([misfit, misfit], 1) * reached)
        store_chunk(back_ref, q, value)
        back_h[slot], back_l[slot] = split(value)

    def fall(q, slot):
        store_chunk(turned, q, dot3((across[0][...], across[1][...]), (back_h[slot], back_l[slot])))

    in_step([(reach, 2), (bend_hidden, 3), (withdraw, 4), (rise, 0), (bend, 1), (fall, 5)])
    place_modes(spectra_of(turned[...], depth), send_ref)


def back_body(near, fetch, outs, put, scratch):
    pre, high, low, turned, *deep = scratch
    depth, back, across = [fetch(k) for k in range(4)], [fetch(4), fetch(5)], [fetch(7), fetch(8)]
    state_ref, slope_ref, mix_h, mix_l = fetch(6), fetch(9), fetch(10), fetch(11)
    deep_cells(near[0], depth, deep)

    def rise(q, slot):
        cells = dot3((back[0][...], back[1][...]), tuple(chunk(part, q) for part in deep))
        pre[slot] = cells + dot3(split(chunk(state_ref, q)), (mix_h[...], mix_l[...]))

    def bend(q, slot):
        for rows, here, there in strips(q):
            high[slot, rows, here], low[slot, rows, here] = split(slope_ref[rows, there] * pre[slot, rows, here])

    def fall(q, slot):
        store_chunk(turned, q, dot3((across[0][...], across[1][...]), (high[slot], low[slot])))

    in_step([(rise, 0), (fall, 2), (bend, 1)])
    place_modes(spectra_of(turned[...], depth), outs[0])


def depth_weight():
    lane = lax.broadcasted_iota(jnp.int32, (1, 128), 1)
    first = lax.rem(lax.axis_index("sp"), 2) * 128
    return jnp.where(lane + first < 16, 1.0, 2.0)


def mode_rows(recv_ref, first, factor, rows_ref):
    spectrum = dot3((first[0][...], first[1][...]), split(recv_ref[...]))
    if factor is not None:
        spectrum = spectrum * factor
    lane = lax.broadcasted_iota(jnp.int32, (64, 128), 1)
    for kz in range(8):
        first = spectrum[:64] if kz == 0 else pltpu.roll(spectrum[:64], 128 - 16 * kz, 1)
        second = spectrum[64:] if kz == 1 else pltpu.roll(spectrum[64:], (144 - 16 * kz) % 128, 1)
        joined = jnp.where(lane < 16, first, jnp.where(lane < 32, second, 0.0))
        rows_ref[pl.ds(kz, 64, stride=8), :] = joined


def selected(rows, table):
    high, low = split(rows)
    return dot(high, table[...]) + dot(low, table[...])


def mode_parts(part):
    return [slice(start + part * 64, start + part * 64 + 64) for start in (0, 256)]


def mode_tiles(part, rows):
    for start in range(part * 64, part * 64 + 64, rows):
        yield slice(start, start + rows), slice(256 + start, 256 + start + rows)


def widen_modes(rows_ref, table, wide):
    def stage(part, slot):
        for rows in mode_parts(part):
            wide[rows, :] = selected(rows_ref[rows, :], table)

    return stage


def send_cells(sums_ref, factor, first_back, send_ref):
    kz_lane = lax.broadcasted_iota(jnp.int32, (64, 128), 1) // 16
    packed = [jnp.zeros((64, 128), f32) for _ in range(2)]
    for kz in range(8):
        for g in range(2):
            packed[g] = jnp.where(kz_lane == kz, sums_ref[pl.ds(g * 512 + kz, 64, stride=8), :], packed[g])
    joined = jnp.concatenate(packed, 0)
    if factor is not None:
        joined = joined * factor
    send_ref[...] = dot3((first_back[0][...], first_back[1][...]), split(joined))


def mix_body(near, fetch, outs, put, scratch):
    send_ref, rows_ref = outs
    wide, sums, out = scratch
    mode_rows(near[0], [fetch(0), fetch(1)], None, rows_ref)
    put(1)
    spread, weight_ref, gather = fetch(2), fetch(3), fetch(4)

    def multiply(part, slot):
        for real, imag in mode_tiles(part, 8):
            total_real = jnp.zeros((8, 128), f32)
            total_imag = jnp.zeros((8, 128), f32)
            for b in range(8):
                columns = slice(b * 128, b * 128 + 128)
                fr, fi = wide[real, columns], wide[imag, columns]
                wr, wi = weight_ref[real, columns], weight_ref[imag, columns]
                total_real = total_real + (fr * wr - fi * wi)
                total_imag = total_imag + (fr * wi + fi * wr)
            sums[real, :] = total_real
            sums[imag, :] = total_imag

    def collect(part, slot):
        for rows in mode_parts(part):
            mixed = selected(sums[rows, :], gather)
            out[rows, :] = mixed[:, :128]
            out[512 + rows.start : 512 + rows.stop, :] = mixed[:, 128:]

    in_step([(widen_modes(rows_ref, spread, wide), 0), (collect, 2), (multiply, 1)], 4)
    send_cells(out, depth_weight(), [fetch(5), fetch(6)], send_ref)


def adjoint_body(near, fetch, outs, put, scratch):
    send_ref, rows_ref = outs
    wide, high, low, out = scratch
    mode_rows(near[0], [fetch(0), fetch(1)], depth_weight(), rows_ref)
    put(1)
    wide[...] = selected(rows_ref[...], fetch(2))
    weight_ref, gather = fetch(3), fetch(4)

    def multiply(part, slot):
        for real, imag in mode_tiles(part, 16):
            br, bi = wide[real, :], wide[imag, :]
            for b in range(8):
                columns = slice(b * 128, b * 128 + 128)
                wr, wi = weight_ref[real, columns], weight_ref[imag, columns]
                high[real, columns], low[real, columns] = split(br * wr + bi * wi)
                high[imag, columns], low[imag, columns] = split(bi * wr - br * wi)

    def collect(part, slot):
        for rows in mode_parts(part):
            mixed = dot(high[rows, :], gather[...]) + dot(low[rows, :], gather[...])
            out[rows, :] = mixed[:, :128]
            out[512 + rows.start : 512 + rows.stop, :] = mixed[:, 128:]

    in_step([(collect, 1), (multiply, 0)], 4)
    send_cells(out, None, [fetch(5), fetch(6)], send_ref)


def outer_products(forward_ref, back_ref, spread_ref, tile_ref, grad_ref, put, wide, narrow):
    narrow[...] = selected(back_ref[...], tile_ref)

    def multiply(part, slot):
        for real, imag in mode_tiles(part, 8):
            br, bi = narrow[real, :], narrow[imag, :]
            for b in range(8):
                columns = slice(b * 128, b * 128 + 128)
                fr, fi = wide[real, columns], wide[imag, columns]
                grad_ref[real, columns] = fr * br + fi * bi
                grad_ref[imag, columns] = fr * bi - fi * br
        for rows in mode_parts(part):
            put(0, pl.ds(rows.start, 64))

    in_step([(widen_modes(forward_ref, spread_ref, wide), 0), (multiply, 1)], 4)


def grad_body(near, fetch, outs, put, scratch):
    outer_products(fetch(0), fetch(1), fetch(2), fetch(3), outs[0], put, *scratch)


def last_body(near, fetch, outs, put, scratch):
    rows, wide, narrow = scratch
    mode_rows(near[0], [fetch(0), fetch(1)], depth_weight(), rows)
    outer_products(fetch(2), rows, fetch(3), fetch(4), outs[0], put, wide, narrow)


def table_body(near, fetch, outs, put, scratch):
    point_one, point_two, hidden_t, hidden_bias, output, bias_one, bias_two, channels, hidden, target, cells = [
        fetch(k) for k in range(11)
    ]
    two_h, two_l, back_h, back_l, up_h, up_l, down_h, down_l, rows_ref, bias_ref, target_ref, local_ref = outs
    one_h, one_l = scratch
    z_row = lax.broadcasted_iota(jnp.int32, (256, 1024), 0) // 16 % 8
    z_column = lax.broadcasted_iota(jnp.int32, (256, 1024), 1) // 16 % 8
    same = z_row == z_column

    def widen(left, right, mask, high, low):
        for part, out in zip(split(left), (high, low)):
            rows = dot(channels[...], part).astype(bf16)
            out[...] = jnp.where(mask, right(rows), 0.0).astype(bf16)

    square = same[:, :256]
    to_channels = lambda rows: dot_t(rows, channels[...])
    to_hidden = lambda rows: dot(rows, hidden[...])
    widen(point_one[...].T, to_channels, square, one_h, one_l)
    widen(point_two[...].T, to_channels, square, two_h, two_l)
    widen(point_two[...], to_channels, square, back_h, back_l)
    widen(hidden_t[...], to_hidden, same, up_h, up_l)
    widen(hidden_t[...] * (0.5 * output[...]), to_hidden, same, down_h, down_l)

    def exact(values, product):
        high, low = split(values)
        last = (values - high.astype(f32) - low.astype(f32)).astype(bf16)
        return product(high) + (product(low) + product(last))

    rows_ref[0:16, :] = exact(jnp.broadcast_to(hidden_bias[...], (16, 128)), to_hidden)
    rows_ref[16:32, :] = exact(jnp.broadcast_to(0.5 * output[...], (16, 128)), to_hidden)
    bias_ref[...] = exact(jnp.broadcast_to(bias_two[...], (8, 32)), to_channels)
    spread = exact(target[...], lambda part: dot(part, cells[...]))
    target_ref[:128, :] = spread[:, :1024]
    target_ref[128:, :] = spread[:, 1024:]
    for k in range(11):
        put(k)
    turned = []
    for g in range(2):
        high, low = split(plain_rows(fetch(11), g * 16, 8))
        turned.append((dot(high, fetch(12)[...]).astype(bf16), dot(low, fetch(12)[...]).astype(bf16)))
    parts = tuple(jnp.concatenate([turned[0][k], turned[1][k]], 1) for k in range(2))
    bias = exact(jnp.broadcast_to(bias_one[...], (8, 32)), to_channels)[:1]
    point_chunks(lambda q: tuple(both(part, q) for part in parts), (one_h[...], one_l[...]), bias, local_ref)
    put(11)


def shards(
    lifted_field,
    target_field,
    spectral_one,
    spectral_two,
    pointwise_one,
    layer_bias_one,
    pointwise_two,
    layer_bias_two,
    hidden_weight,
    hidden_bias,
    output_weight,
):
    across = tuple(map(jnp.asarray, two_parts(across_table())))
    across_back = tuple(map(jnp.asarray, two_parts(np.ascontiguousarray(across_table().T))))
    depth, depth_lifted = (
        tuple(jnp.asarray(part) for wave in depth_table(major) for part in two_parts(wave)) for major in (False, True)
    )
    first = tuple(map(jnp.asarray, two_parts(first_table())))
    first_back = tuple(map(jnp.asarray, two_parts(np.ascontiguousarray(first_table().T))))
    spread, tile, gather, gather_rows = map(jnp.asarray, selectors())
    channels, hidden, ones, cells = map(jnp.asarray, head_selectors())
    turn = jnp.asarray(turn_table())

    field = lifted_field.reshape(W, 2, 64, 128).transpose(0, 2, 1, 3).reshape(W, 128, 128)
    target = target_field.reshape(2, 64, 128).transpose(1, 0, 2).reshape(128, 128)
    weights_one = spectral_one.reshape(512, 1024)
    weights_two = spectral_two.reshape(512, 1024)
    def exchange(blocks):
        moved = lax.all_to_all(blocks.reshape(64, 8, 128), "sp", split_axis=0, concat_axis=0, tiled=True)
        return moved.reshape(512, 128)

    block, grid, wide = (512, 128), (256, 2048), (512, 1024)
    vm = pltpu.VMEM
    near_out = (block, f32, "near")
    far_out = lambda shape, kind=f32: (shape, kind, "far")
    pair = lambda lanes, kind: vm((2, 256, lanes), kind)
    work = [pair(256, f32), pair(256, bf16), pair(256, bf16), vm((128, 2048), f32), vm((128, 2048), bf16), vm((128, 2048), bf16)]
    mix_work = [vm(wide, f32), vm(block, f32), vm((1024, 128), f32)]

    (send,) = run(
        lift_body, "lift", 2 * 10**9, (), (*across, *[field] * 4, *depth_lifted), [near_out], [],
        parts={2 + part: (8 * part, 8 * part + 8) for part in range(4)},
    )
    recv = exchange(send)
    row = lambda vector: vector.reshape(1, -1)
    made = run(
        table_body, "tables", 6 * 10**9, (),
        (
            pointwise_one, pointwise_two, hidden_weight.T, row(hidden_bias), row(output_weight),
            row(layer_bias_one), row(layer_bias_two), channels, hidden, target, cells, field, turn,
        ),
        [far_out((256, 256), bf16)] * 4 + [far_out((256, 1024), bf16)] * 4
        + [far_out((32, 1024)), far_out((8, 256)), far_out((256, 1024)), far_out(grid)],
        [vm((256, 256), bf16), vm((256, 256), bf16)],
    )
    mix_two, mix_back, up, down = made[0:2], made[2:4], made[4:6], made[6:8]
    hidden_rows, bias_two, target_wide, local_one = made[8:]
    send, modes_one = run(
        mix_body, "mix_one", 10**9, (recv,), (*first, spread, weights_one, gather, *first_back, bias_two),
        [near_out, (block, f32, "kept")], mix_work, managed=True, fetched=(4, 7),
    )
    recv = exchange(send)
    send, state_one, slope_one = run(
        one_body, "grid_one", 5 * 10**9, (recv,), (*depth, *across_back, local_one, *across),
        [near_out, far_out(grid), far_out(grid)], work, managed=True, fetched=(6,),
    )
    recv = exchange(send)
    send, modes_two = run(
        mix_body, "mix_two", 10**9, (recv,), (*first, spread, weights_two, gather, *first_back),
        [near_out, far_out(block)], mix_work, managed=True,
    )
    recv = exchange(send)
    send, back_two = run(
        two_body, "grid_two", 15 * 10**9, (recv,),
        (*depth, *across_back, state_one, *across, *up, hidden_rows, *down, ones, target_wide, *mix_two, bias_two),
        [near_out, far_out(grid)],
        work
        + [vm(grid, f32), pair(1024, f32), pair(1024, bf16), pair(1024, bf16), pair(256, bf16), pair(256, bf16), pair(256, bf16)],
        managed=True,
    )
    recv = exchange(send)
    send, modes_back = run(
        adjoint_body, "adjoint", 10**9, (recv,), (*first, tile, weights_two, gather_rows, *first_back),
        [near_out, far_out(block)], [vm(block, f32), vm(wide, bf16), vm(wide, bf16), vm((1024, 128), f32)],
        managed=True,
    )
    recv = exchange(send)
    (gradient_two,) = run(
        grad_body, "grad_two", 10**9, (), (modes_two, modes_back, spread, tile), [far_out(wide)], [vm(wide, f32), vm(block, f32)]
    )
    (send,) = run(
        back_body, "grid_back", 5 * 10**9, (recv,), (*depth, *across_back, back_two, *across, slope_one, *mix_back), [near_out], work, managed=True,
    )
    recv = exchange(send)
    (gradient_one,) = run(
        last_body, "grad_one", 10**9, (recv,), (*first, modes_one, spread, tile), [far_out(wide)],
        [vm(block, f32), vm(wide, f32), vm(block, f32)],
    )
    shape = (2, KX, 8, W * W)
    return (gradient_one.reshape(shape), gradient_two.reshape(shape))


def solution(mesh):
    in_specs = (
        P("batch", "sp", None),
        P("sp", "batch"),
        P(None, None, "sp", None),
        P(None, None, "sp", None),
        P(),
        P(),
        P(),
        P(),
        P(),
        P(),
        P(),
    )
    out_specs = (P("batch", None, "sp", None), P("batch", None, "sp", None))
    return jax.shard_map(shards, mesh=mesh, in_specs=in_specs, out_specs=out_specs, check_vma=False)
```

```python
import jax
import jax.numpy as jnp
import ml_dtypes
import numpy as np
from jax import lax
from jax.experimental import pallas as pl
from jax.experimental.pallas import tpu as pltpu
from jax.sharding import PartitionSpec as P

W = 32
H = 128
NX = 128
NY = 128
NZ = 64
KX = 32
KY = 32
KZ = 16

f32 = jnp.float32
bf16 = jnp.bfloat16
ROOT = 0.7978845608028654
CUBE = 0.044715 * ROOT


def centred(number, length):
    indices = np.arange(number)
    return np.where(indices < number // 2, indices, length - number + indices)


def two_parts(table):
    high = table.astype(ml_dtypes.bfloat16)
    low = (table - high.astype(np.float64)).astype(ml_dtypes.bfloat16)
    return high, low


def across_table():
    y = 2 * np.arange(64)[None, :] + np.arange(2)[:, None]
    angle = 2 * np.pi * (centred(KY, NY)[:, None, None] * y[None] % NY) / NY
    waves = np.stack([np.cos(angle), -np.sin(angle)])
    return np.einsum("skab,rt->srkabt", waves, np.eye(2)).reshape(128, 256)


def rotation(angle):
    cosine, sine = np.cos(angle), np.sin(angle)
    return np.stack([np.stack([cosine, -sine]), np.stack([sine, cosine])])


def depth_table(channel_major):
    angle = 2 * np.pi * (np.arange(NZ)[:, None] * np.arange(KZ)[None] % NZ) / NZ
    form = "zk,cd->czkd" if channel_major else "zk,cd->zckd"
    return [np.einsum(form, wave(angle), np.eye(16)).reshape(1024, 256) for wave in (np.cos, np.sin)]


def first_table():
    places = 2 * np.arange(64)[:, None] + np.arange(2)[None]
    angle = 2 * np.pi * (centred(KX, NX)[:, None, None] * places[None] % NX) / NX
    table = np.einsum("stkdr,gh->gtkdrsh", rotation(angle), np.eye(2))
    return table.reshape(128, 512) / 1024.0


def selectors():
    eye16, eye32 = np.eye(16), np.eye(32)
    lanes = np.zeros((128, 32))
    lanes[:32] = eye32
    spread = np.einsum("li,o->lio", lanes, np.ones(32)).reshape(128, 1024)
    tile = np.einsum("lo,i->lio", lanes, np.ones(4)).reshape(128, 128)
    halves = eye32.reshape(32, 2, 16)
    gather = np.einsum("i,ogc,k->iogkc", np.ones(4), halves, np.ones(8)).reshape(128, 256)
    gather_rows = np.einsum("igc,o,k->iogkc", halves, np.ones(32), np.ones(8)).reshape(1024, 256)
    return [part.astype(ml_dtypes.bfloat16) for part in (spread, tile, gather, gather_rows)]


def head_selectors():
    one = ml_dtypes.bfloat16
    channels = np.einsum("z,igc->gzci", np.ones(8), np.eye(32).reshape(32, 2, 16)).reshape(256, 32)
    hidden = np.einsum("hbu,z->hbzu", np.eye(128).reshape(128, 8, 16), np.ones(8)).reshape(128, 1024)
    ones = np.einsum("zy,uc->zuyc", np.eye(8), np.ones((16, 16))).reshape(128, 128)
    cells = np.einsum("ab,zy,c->bzayc", np.eye(2), np.eye(64), np.ones(16)).reshape(128, 2048)
    return channels.astype(one), hidden.astype(one), ones.astype(one), cells.astype(one)


def turn_table():
    return np.einsum("zy,cd->czyd", np.eye(64), np.eye(16)).reshape(1024, 1024).astype(ml_dtypes.bfloat16)


def split(values):
    high = values.astype(bf16)
    return high, (values - high.astype(f32)).astype(bf16)


def dot(left, right):
    return lax.dot_general(left, right, (((1,), (0,)), ((), ())), preferred_element_type=f32)


def dot_t(left, right):
    return lax.dot_general(left, right, (((1,), (1,)), ((), ())), preferred_element_type=f32)


def dot3(left, right, product=dot):
    return product(left[0], right[0]) + (product(left[1], right[0]) + product(left[0], right[1]))


def run(body, name, flops, near, far, outs, scratch, parts={}, managed=False, fetched=()):
    mine = list(fetched) if managed else list(range(len(far)))
    if managed:
        outs = [(shape, kind, "near" if place == "far" else place) for shape, kind, place in outs]
    leaving = [k for k, out in enumerate(outs) if out[2] != "near"]

    def kernel(*refs):
        refs = list(refs)
        take = lambda count: [refs.pop(0) for _ in range(count)]
        near_refs, far_refs, out_refs = take(len(near)), take(len(far)), take(len(outs))
        copied, filled = dict(zip(mine, take(len(mine)))), take(len(leaving))
        scratch_refs = take(len(scratch))
        arrived, left = refs
        for k, (start, stop) in parts.items():
            far_refs[k] = far_refs[k].at[pl.ds(start, stop - start)]
        copies = {k: pltpu.make_async_copy(far_refs[k], copied[k], arrived.at[k]) for k in mine}
        for copy in copies.values():
            copy.start()
        waited, started = set(), []

        def fetch(k):
            if k not in copies:
                return far_refs[k]
            if k not in waited:
                copies[k].wait()
                waited.add(k)
            return copied[k]

        def put(k, rows=None):
            if k not in leaving:
                return
            source, target = filled[leaving.index(k)], out_refs[k]
            if rows is not None:
                source, target = source.at[rows], target.at[rows]
            copy = pltpu.make_async_copy(source, target, left.at[len(started)])
            copy.start()
            started.append(copy)

        shown = [filled[leaving.index(k)] if k in leaving else out for k, out in enumerate(out_refs)]
        body(near_refs, fetch, shown, put, scratch_refs)
        for k in range(len(far)):
            fetch(k)
        for copy in started:
            copy.wait()

    far = [pltpu.with_memory_space_constraint(o, pltpu.HBM) if k in mine else o for k, o in enumerate(far)]
    vmem, hbm = pl.BlockSpec(memory_space=pltpu.VMEM), pl.BlockSpec(memory_space=pltpu.HBM)
    moved = sum(o.size * o.dtype.itemsize for o in (*near, *far))
    return pl.pallas_call(
        kernel,
        in_specs=[vmem] * len(near) + [hbm if k in mine else vmem for k in range(len(far))],
        out_specs=[vmem if out[2] == "near" else hbm for out in outs],
        out_shape=[jax.ShapeDtypeStruct(out[0], out[1]) if out[2] == "near" else pltpu.HBM(out[0], out[1]) for out in outs],
        scratch_shapes=[
            pltpu.VMEM((parts[k][1] - parts[k][0], *o.shape[1:]) if k in parts else o.shape, o.dtype)
            for k, o in enumerate(far)
            if k in mine
        ]
        + [pltpu.VMEM(outs[k][0], outs[k][1]) for k in leaving]
        + scratch
        + [pltpu.SemaphoreType.DMA((max(1, len(far)),)), pltpu.SemaphoreType.DMA((16,))],
        name=name,
        cost_estimate=pl.CostEstimate(flops=flops, bytes_accessed=int(moved), transcendentals=0),
        compiler_params=pltpu.CompilerParams(vmem_limit_bytes=28 * 1024 * 1024),
    )(*near, *far)


def spectra_of(turned, depth):
    rows = [turned[s * 64 : s * 64 + 64, g * 1024 : g * 1024 + 1024] for s in range(2) for g in range(2)]
    left = split(jnp.concatenate(rows, 0))
    even = dot3(left, (depth[0][...], depth[1][...]))
    odd = dot3(left, (depth[2][...], depth[3][...]))
    return even[:128] + odd[128:], even[128:] - odd[:128]


def place_modes(spectra, send_ref):
    for p in range(2):
        for g in range(2):
            for r in range(2):
                for kzh in range(2):
                    row = g * 64 + r * 32
                    send_ref[pl.ds(kzh * 8 + r * 4 + p * 2 + g, 32, stride=16), :] = spectra[p][
                        row : row + 32, kzh * 128 : kzh * 128 + 128
                    ]


def taken_rows(recv_ref):
    rows = []
    for p in range(2):
        for g in range(2):
            for r in range(2):
                pieces = [recv_ref[pl.ds(kzh * 8 + r * 4 + p * 2 + g, 32, stride=16), :] for kzh in range(2)]
                rows.append(jnp.concatenate(pieces, 1))
    return split(jnp.concatenate(rows, 0))


def deep_cells(recv_ref, depth, deep):
    left = taken_rows(recv_ref)
    even = dot3(left, (depth[0][...], depth[1][...]), dot_t)
    odd = dot3(left, (depth[2][...], depth[3][...]), dot_t)
    for p, part in enumerate((even[:128] - odd[128:], odd[:128] + even[128:])):
        for g in range(2):
            rows, lanes = slice(p * 64, p * 64 + 64), slice(g * 1024, g * 1024 + 1024)
            deep[0][rows, lanes], deep[1][rows, lanes] = split(part[g * 64 : g * 64 + 64])


def chunk(ref, q):
    return jnp.concatenate([ref[:, q * 128 : q * 128 + 128], ref[:, 1024 + q * 128 : 1152 + q * 128]], 1)


def store_chunk(ref, q, value):
    ref[:, q * 128 : q * 128 + 128] = value[:, :128]
    ref[:, 1024 + q * 128 : 1152 + q * 128] = value[:, 128:]


def strips(q):
    for start in range(0, 256, 16):
        for g in range(2):
            place = g * 1024 + q * 128
            yield slice(start, start + 16), slice(g * 128, g * 128 + 128), slice(place, place + 128)


def in_step(stages, count=8):
    for i in range(count + max(lag for _, lag in stages)):
        for stage, lag in stages:
            if 0 <= i - lag < count:
                stage(i - lag, (i - lag) % 2)


def plain_rows(field_ref, start, pairs):
    low_rows, high_rows = [], []
    lane = lax.broadcasted_iota(jnp.int32, (128, 128), 1) < 64
    for pair in range(pairs):
        first = field_ref[start + 2 * pair]
        second = field_ref[start + 2 * pair + 1]
        low_rows.append(jnp.where(lane, first, pltpu.roll(second, 64, 1)))
        high_rows.append(jnp.where(lane, pltpu.roll(first, 64, 1), second))
    return jnp.concatenate([jnp.concatenate(low_rows, 1), jnp.concatenate(high_rows, 1)], 0)


def lift_body(near, fetch, outs, put, scratch):
    across = (fetch(0)[...], fetch(1)[...])
    turned = [dot3(across, split(plain_rows(fetch(2 + part), 0, 8))) for part in range(2)]
    place_modes(spectra_of(jnp.concatenate(turned, 1), [fetch(k) for k in range(4, 8)]), outs[0])


def point_chunks(parts_at, mix, bias, out_ref):
    for q in range(8):
        mixed = dot3(parts_at(q), mix) + bias
        out_ref[:, q * 128 : q * 128 + 128] = mixed[:, :128]
        out_ref[:, 1024 + q * 128 : 1152 + q * 128] = mixed[:, 128:]


def both(value, q):
    return jnp.concatenate([value[:, q * 128 : q * 128 + 128], value[:, 1024 + q * 128 : 1152 + q * 128]], 1)


def gelu_parts(x):
    square = x * x
    cubic = square * CUBE
    bend = jnp.tanh(x * (cubic + ROOT))
    above = bend + 1.0
    twice = x * above
    slope = above + (twice * (1.0 - bend)) * (cubic * 3.0 + ROOT)
    return twice, slope


def one_body(near, fetch, outs, put, scratch):
    send_ref, state_ref, slope_ref = outs
    pre, high, low, turned, *deep = scratch
    depth, back, across = [fetch(k) for k in range(4)], [fetch(4), fetch(5)], [fetch(7), fetch(8)]
    deep_cells(near[0], depth, deep)
    local_ref = fetch(6)

    def rise(q, slot):
        pre[slot] = dot3((back[0][...], back[1][...]), tuple(chunk(part, q) for part in deep))

    def bend(q, slot):
        for rows, here, there in strips(q):
            twice, slope = gelu_parts(pre[slot, rows, here] + local_ref[rows, there])
            state = 0.5 * twice
            state_ref[rows, there] = state
            slope_ref[rows, there] = 0.5 * slope
            high[slot, rows, here], low[slot, rows, here] = split(state)

    def fall(q, slot):
        store_chunk(turned, q, dot3((across[0][...], across[1][...]), (high[slot], low[slot])))

    in_step([(rise, 0), (fall, 2), (bend, 1)])
    place_modes(spectra_of(turned[...], depth), send_ref)


def two_body(near, fetch, outs, put, scratch):
    send_ref, back_ref = outs
    pre, high, low, turned, deep_h, deep_l, slopes, hidden, slope_h, slope_l, sums, back_h, back_l = scratch
    depth, back, across = [fetch(k) for k in range(4)], [fetch(4), fetch(5)], [fetch(7), fetch(8)]
    up_h, up_l, rows_ref, down_h, down_l, ones_ref, target_ref = [fetch(k) for k in range(9, 16)]
    state_ref, mix_h, mix_l, bias_ref = fetch(6), fetch(16), fetch(17), fetch(18)
    deep_cells(near[0], depth, (deep_h, deep_l))

    def rise(q, slot):
        cells = dot3((back[0][...], back[1][...]), (chunk(deep_h, q), chunk(deep_l, q)))
        local = dot3(split(chunk(state_ref, q)), (mix_h[...], mix_l[...]))
        pre[slot] = cells + (local + bias_ref[:1, :])

    def bend(q, slot):
        for rows, here, there in strips(q):
            twice, slope = gelu_parts(pre[slot, rows, here])
            slopes[rows, there] = 0.5 * slope
            high[slot, rows, here], low[slot, rows, here] = split(0.5 * twice)

    def reach(q, slot):
        hidden[slot] = dot3((high[slot], low[slot]), (up_h[...], up_l[...]))

    def bend_hidden(q, slot):
        for start in range(0, 256, 16):
            rows = slice(start, start + 16)
            total = jnp.zeros((16, 128), f32)
            for b in range(8):
                columns = slice(b * 128, b * 128 + 128)
                twice, slope = gelu_parts(hidden[slot, rows, columns] + rows_ref[0:16, columns])
                total = total + twice * rows_ref[16:32, columns]
                slope_h[slot, rows, columns], slope_l[slot, rows, columns] = split(slope)
            sums[slot, rows, :128], sums[slot, rows, 128:] = split(total)

    def withdraw(q, slot):
        reached = dot3((slope_h[slot], slope_l[slot]), (down_h[...], down_l[...]), dot_t)
        misfit = dot(sums[slot, :, :128], ones_ref[...]) + dot(sums[slot, :, 128:], ones_ref[...])
        misfit = misfit - target_ref[:, q * 128 : q * 128 + 128]
        value = chunk(slopes, q) * (jnp.concatenate([misfit, misfit], 1) * reached)
        store_chunk(back_ref, q, value)
        back_h[slot], back_l[slot] = split(value)

    def fall(q, slot):
        store_chunk(turned, q, dot3((across[0][...], across[1][...]), (back_h[slot], back_l[slot])))

    in_step([(reach, 2), (bend_hidden, 3), (withdraw, 4), (rise, 0), (bend, 1), (fall, 5)])
    place_modes(spectra_of(turned[...], depth), send_ref)


def back_body(near, fetch, outs, put, scratch):
    pre, high, low, turned, *deep = scratch
    depth, back, across = [fetch(k) for k in range(4)], [fetch(4), fetch(5)], [fetch(7), fetch(8)]
    state_ref, slope_ref, mix_h, mix_l = fetch(6), fetch(9), fetch(10), fetch(11)
    deep_cells(near[0], depth, deep)

    def rise(q, slot):
        cells = dot3((back[0][...], back[1][...]), tuple(chunk(part, q) for part in deep))
        pre[slot] = cells + dot3(split(chunk(state_ref, q)), (mix_h[...], mix_l[...]))

    def bend(q, slot):
        for rows, here, there in strips(q):
            high[slot, rows, here], low[slot, rows, here] = split(slope_ref[rows, there] * pre[slot, rows, here])

    def fall(q, slot):
        store_chunk(turned, q, dot3((across[0][...], across[1][...]), (high[slot], low[slot])))

    in_step([(rise, 0), (fall, 2), (bend, 1)])
    place_modes(spectra_of(turned[...], depth), outs[0])


def depth_weight():
    lane = lax.broadcasted_iota(jnp.int32, (1, 128), 1)
    first = lax.rem(lax.axis_index("sp"), 2) * 128
    return jnp.where(lane + first < 16, 1.0, 2.0)


def mode_rows(recv_ref, first, factor, rows_ref):
    spectrum = dot3((first[0][...], first[1][...]), split(recv_ref[...]))
    if factor is not None:
        spectrum = spectrum * factor
    lane = lax.broadcasted_iota(jnp.int32, (64, 128), 1)
    for kz in range(8):
        first = spectrum[:64] if kz == 0 else pltpu.roll(spectrum[:64], 128 - 16 * kz, 1)
        second = spectrum[64:] if kz == 1 else pltpu.roll(spectrum[64:], (144 - 16 * kz) % 128, 1)
        joined = jnp.where(lane < 16, first, jnp.where(lane < 32, second, 0.0))
        rows_ref[pl.ds(kz, 64, stride=8), :] = joined


def selected(rows, table):
    high, low = split(rows)
    return dot(high, table[...]) + dot(low, table[...])


def mode_parts(part):
    return [slice(start + part * 64, start + part * 64 + 64) for start in (0, 256)]


def mode_tiles(part, rows):
    for start in range(part * 64, part * 64 + 64, rows):
        yield slice(start, start + rows), slice(256 + start, 256 + start + rows)


def widen_modes(rows_ref, table, wide):
    def stage(part, slot):
        for rows in mode_parts(part):
            wide[rows, :] = selected(rows_ref[rows, :], table)

    return stage


def send_cells(sums_ref, factor, first_back, send_ref):
    kz_lane = lax.broadcasted_iota(jnp.int32, (64, 128), 1) // 16
    packed = [jnp.zeros((64, 128), f32) for _ in range(2)]
    for kz in range(8):
        for g in range(2):
            packed[g] = jnp.where(kz_lane == kz, sums_ref[pl.ds(g * 512 + kz, 64, stride=8), :], packed[g])
    joined = jnp.concatenate(packed, 0)
    if factor is not None:
        joined = joined * factor
    send_ref[...] = dot3((first_back[0][...], first_back[1][...]), split(joined))


def mix_body(near, fetch, outs, put, scratch):
    send_ref, rows_ref = outs
    wide, sums, out = scratch
    mode_rows(near[0], [fetch(0), fetch(1)], None, rows_ref)
    put(1)
    spread, weight_ref, gather = fetch(2), fetch(3), fetch(4)

    def multiply(part, slot):
        for real, imag in mode_tiles(part, 8):
            total_real = jnp.zeros((8, 128), f32)
            total_imag = jnp.zeros((8, 128), f32)
            for b in range(8):
                columns = slice(b * 128, b * 128 + 128)
                fr, fi = wide[real, columns], wide[imag, columns]
                wr, wi = weight_ref[real, columns], weight_ref[imag, columns]
                total_real = total_real + (fr * wr - fi * wi)
                total_imag = total_imag + (fr * wi + fi * wr)
            sums[real, :] = total_real
            sums[imag, :] = total_imag

    def collect(part, slot):
        for rows in mode_parts(part):
            mixed = selected(sums[rows, :], gather)
            out[rows, :] = mixed[:, :128]
            out[512 + rows.start : 512 + rows.stop, :] = mixed[:, 128:]

    in_step([(widen_modes(rows_ref, spread, wide), 0), (collect, 2), (multiply, 1)], 4)
    send_cells(out, depth_weight(), [fetch(5), fetch(6)], send_ref)


def adjoint_body(near, fetch, outs, put, scratch):
    send_ref, rows_ref = outs
    wide, high, low, out = scratch
    mode_rows(near[0], [fetch(0), fetch(1)], depth_weight(), rows_ref)
    put(1)
    wide[...] = selected(rows_ref[...], fetch(2))
    weight_ref, gather = fetch(3), fetch(4)

    def multiply(part, slot):
        for real, imag in mode_tiles(part, 16):
            br, bi = wide[real, :], wide[imag, :]
            for b in range(8):
                columns = slice(b * 128, b * 128 + 128)
                wr, wi = weight_ref[real, columns], weight_ref[imag, columns]
                high[real, columns], low[real, columns] = split(br * wr + bi * wi)
                high[imag, columns], low[imag, columns] = split(bi * wr - br * wi)

    def collect(part, slot):
        for rows in mode_parts(part):
            mixed = dot(high[rows, :], gather[...]) + dot(low[rows, :], gather[...])
            out[rows, :] = mixed[:, :128]
            out[512 + rows.start : 512 + rows.stop, :] = mixed[:, 128:]

    in_step([(collect, 1), (multiply, 0)], 4)
    send_cells(out, None, [fetch(5), fetch(6)], send_ref)


def outer_products(forward_ref, back_ref, spread_ref, tile_ref, grad_ref, put, wide, narrow):
    narrow[...] = selected(back_ref[...], tile_ref)

    def multiply(part, slot):
        for real, imag in mode_tiles(part, 8):
            br, bi = narrow[real, :], narrow[imag, :]
            for b in range(8):
                columns = slice(b * 128, b * 128 + 128)
                fr, fi = wide[real, columns], wide[imag, columns]
                grad_ref[real, columns] = fr * br + fi * bi
                grad_ref[imag, columns] = fr * bi - fi * br
        for rows in mode_parts(part):
            put(0, pl.ds(rows.start, 64))

    in_step([(widen_modes(forward_ref, spread_ref, wide), 0), (multiply, 1)], 4)


def grad_body(near, fetch, outs, put, scratch):
    outer_products(fetch(0), fetch(1), fetch(2), fetch(3), outs[0], put, *scratch)


def last_body(near, fetch, outs, put, scratch):
    rows, wide, narrow = scratch
    mode_rows(near[0], [fetch(0), fetch(1)], depth_weight(), rows)
    outer_products(fetch(2), rows, fetch(3), fetch(4), outs[0], put, wide, narrow)


def table_body(near, fetch, outs, put, scratch):
    point_one, point_two, hidden_t, hidden_bias, output, bias_one, bias_two, channels, hidden, target, cells = [
        fetch(k) for k in range(11)
    ]
    two_h, two_l, back_h, back_l, up_h, up_l, down_h, down_l, rows_ref, bias_ref, target_ref, local_ref = outs
    one_h, one_l = scratch
    z_row = lax.broadcasted_iota(jnp.int32, (256, 1024), 0) // 16 % 8
    z_column = lax.broadcasted_iota(jnp.int32, (256, 1024), 1) // 16 % 8
    same = z_row == z_column

    def widen(left, right, mask, high, low):
        for part, out in zip(split(left), (high, low)):
            rows = dot(channels[...], part).astype(bf16)
            out[...] = jnp.where(mask, right(rows), 0.0).astype(bf16)

    square = same[:, :256]
    to_channels = lambda rows: dot_t(rows, channels[...])
    to_hidden = lambda rows: dot(rows, hidden[...])
    widen(point_one[...].T, to_channels, square, one_h, one_l)
    widen(point_two[...].T, to_channels, square, two_h, two_l)
    widen(point_two[...], to_channels, square, back_h, back_l)
    widen(hidden_t[...], to_hidden, same, up_h, up_l)
    widen(hidden_t[...] * (0.5 * output[...]), to_hidden, same, down_h, down_l)

    def exact(values, product):
        high, low = split(values)
        last = (values - high.astype(f32) - low.astype(f32)).astype(bf16)
        return product(high) + (product(low) + product(last))

    rows_ref[0:16, :] = exact(jnp.broadcast_to(hidden_bias[...], (16, 128)), to_hidden)
    rows_ref[16:32, :] = exact(jnp.broadcast_to(0.5 * output[...], (16, 128)), to_hidden)
    bias_ref[...] = exact(jnp.broadcast_to(bias_two[...], (8, 32)), to_channels)
    spread = exact(target[...], lambda part: dot(part, cells[...]))
    target_ref[:128, :] = spread[:, :1024]
    target_ref[128:, :] = spread[:, 1024:]
    for k in range(11):
        put(k)
    turned = []
    for g in range(2):
        high, low = split(plain_rows(fetch(11), g * 16, 8))
        turned.append((dot(high, fetch(12)[...]).astype(bf16), dot(low, fetch(12)[...]).astype(bf16)))
    parts = tuple(jnp.concatenate([turned[0][k], turned[1][k]], 1) for k in range(2))
    bias = exact(jnp.broadcast_to(bias_one[...], (8, 32)), to_channels)[:1]
    point_chunks(lambda q: tuple(both(part, q) for part in parts), (one_h[...], one_l[...]), bias, local_ref)
    put(11)


def shards(
    lifted_field,
    target_field,
    spectral_one,
    spectral_two,
    pointwise_one,
    layer_bias_one,
    pointwise_two,
    layer_bias_two,
    hidden_weight,
    hidden_bias,
    output_weight,
):
    across = tuple(map(jnp.asarray, two_parts(across_table())))
    across_back = tuple(map(jnp.asarray, two_parts(np.ascontiguousarray(across_table().T))))
    depth, depth_lifted = (
        tuple(jnp.asarray(part) for wave in depth_table(major) for part in two_parts(wave)) for major in (False, True)
    )
    first = tuple(map(jnp.asarray, two_parts(first_table())))
    first_back = tuple(map(jnp.asarray, two_parts(np.ascontiguousarray(first_table().T))))
    spread, tile, gather, gather_rows = map(jnp.asarray, selectors())
    channels, hidden, ones, cells = map(jnp.asarray, head_selectors())
    turn = jnp.asarray(turn_table())

    field = lifted_field.reshape(W, 2, 64, 128).transpose(0, 2, 1, 3).reshape(W, 128, 128)
    target = target_field.reshape(2, 64, 128).transpose(1, 0, 2).reshape(128, 128)
    weights_one = spectral_one.reshape(512, 1024)
    weights_two = spectral_two.reshape(512, 1024)
    def exchange(blocks):
        moved = lax.all_to_all(blocks.reshape(64, 8, 128), "sp", split_axis=0, concat_axis=0, tiled=True)
        return moved.reshape(512, 128)

    block, grid, wide = (512, 128), (256, 2048), (512, 1024)
    vm = pltpu.VMEM
    near_out = (block, f32, "near")
    far_out = lambda shape, kind=f32: (shape, kind, "far")
    pair = lambda lanes, kind: vm((2, 256, lanes), kind)
    work = [pair(256, f32), pair(256, bf16), pair(256, bf16), vm((128, 2048), f32), vm((128, 2048), bf16), vm((128, 2048), bf16)]
    mix_work = [vm(wide, f32), vm(block, f32), vm((1024, 128), f32)]

    (send,) = run(
        lift_body, "lift", 2 * 10**9, (), (*across, field, field, *depth_lifted), [near_out], [],
        parts={2: (0, 16), 3: (16, 32)},
    )
    recv = exchange(send)
    row = lambda vector: vector.reshape(1, -1)
    made = run(
        table_body, "tables", 6 * 10**9, (),
        (
            pointwise_one, pointwise_two, hidden_weight.T, row(hidden_bias), row(output_weight),
            row(layer_bias_one), row(layer_bias_two), channels, hidden, target, cells, field, turn,
        ),
        [far_out((256, 256), bf16)] * 4 + [far_out((256, 1024), bf16)] * 4
        + [far_out((32, 1024)), far_out((8, 256)), far_out((256, 1024)), far_out(grid)],
        [vm((256, 256), bf16), vm((256, 256), bf16)],
    )
    mix_two, mix_back, up, down = made[0:2], made[2:4], made[4:6], made[6:8]
    hidden_rows, bias_two, target_wide, local_one = made[8:]
    send, modes_one = run(
        mix_body, "mix_one", 10**9, (recv,), (*first, spread, weights_one, gather, *first_back, bias_two),
        [near_out, (block, f32, "kept")], mix_work, managed=True, fetched=(4, 7),
    )
    recv = exchange(send)
    send, state_one, slope_one = run(
        one_body, "grid_one", 5 * 10**9, (recv,), (*depth, *across_back, local_one, *across),
        [near_out, far_out(grid), far_out(grid)], work, managed=True, fetched=(6,),
    )
    recv = exchange(send)
    send, modes_two = run(
        mix_body, "mix_two", 10**9, (recv,), (*first, spread, weights_two, gather, *first_back),
        [near_out, far_out(block)], mix_work, managed=True,
    )
    recv = exchange(send)
    send, back_two = run(
        two_body, "grid_two", 15 * 10**9, (recv,),
        (*depth, *across_back, state_one, *across, *up, hidden_rows, *down, ones, target_wide, *mix_two, bias_two),
        [near_out, far_out(grid)],
        work
        + [vm(grid, f32), pair(1024, f32), pair(1024, bf16), pair(1024, bf16), pair(256, bf16), pair(256, bf16), pair(256, bf16)],
        managed=True,
    )
    recv = exchange(send)
    send, modes_back = run(
        adjoint_body, "adjoint", 10**9, (recv,), (*first, tile, weights_two, gather_rows, *first_back),
        [near_out, far_out(block)], [vm(block, f32), vm(wide, bf16), vm(wide, bf16), vm((1024, 128), f32)],
        managed=True,
    )
    recv = exchange(send)
    (gradient_two,) = run(
        grad_body, "grad_two", 10**9, (), (modes_two, modes_back, spread, tile), [far_out(wide)], [vm(wide, f32), vm(block, f32)]
    )
    (send,) = run(
        back_body, "grid_back", 5 * 10**9, (recv,), (*depth, *across_back, back_two, *across, slope_one, *mix_back), [near_out], work, managed=True,
    )
    recv = exchange(send)
    (gradient_one,) = run(
        last_body, "grad_one", 10**9, (recv,), (*first, modes_one, spread, tile), [far_out(wide)],
        [vm(block, f32), vm(wide, f32), vm(block, f32)],
    )
    shape = (2, KX, 8, W * W)
    return (gradient_one.reshape(shape), gradient_two.reshape(shape))


def solution(mesh):
    in_specs = (
        P("batch", "sp", None),
        P("sp", "batch"),
        P(None, None, "sp", None),
        P(None, None, "sp", None),
        P(),
        P(),
        P(),
        P(),
        P(),
        P(),
        P(),
    )
    out_specs = (P("batch", None, "sp", None), P("batch", None, "sp", None))
    return jax.shard_map(shards, mesh=mesh, in_specs=in_specs, out_specs=out_specs, check_vma=False)
```
